32 devices in a mesh: pipe: 2 (over y), ctx: 4 (over x, core), tp: 4 (over z).
Axes of the slice: x: 2, y: 2, z: 4, core: 2. Of those that a mesh axis runs over, the one named last changes fastest.
Arguments:
- queries: bfloat16 [2, 2048, 4096], P('pipe', 'ctx', 'tp'), may hold values from -24 to 24
- keys: bfloat16 [2, 2048, 4096], P('pipe', 'ctx', 'tp'), may hold values from -24 to 24
- values: bfloat16 [2, 2048, 4096], P('pipe', 'ctx', 'tp'), may hold values from -6 to 6
- stream: bfloat16 [2, 2048, 8192], P('pipe', 'ctx', 'tp'), may hold values from -6 to 6
- grad_stream: bfloat16 [2, 2048, 8192], P('pipe', 'ctx', 'tp'), may hold values from -6 to 6
- out_proj: bfloat16 [2, 4096, 8192], P('pipe', 'tp'), may hold values from -0.09375 to 0.09375
- doc_ids: int32 [2, 2048], P('pipe'), may hold values from 0 to 1, never falling along the last dimension, each value on 1 to 1536 neighbouring positions
Outputs:
- grad_queries: bfloat16 [2, 2048, 4096], P('pipe', 'ctx', 'tp')
- grad_keys: bfloat16 [2, 2048, 4096], P('pipe', 'ctx', 'tp')
- grad_values: bfloat16 [2, 2048, 4096], P('pipe', 'ctx', 'tp')
- next_stream: bfloat16 [2, 2048, 8192], P('pipe', 'ctx', 'tp')
- next_grad: bfloat16 [2, 2048, 8192], P('pipe', 'ctx', 'tp')
The draws below stay inside these ranges and needn't reach their ends.
Inputs may be any that keep to these rules, and one draw needn't show every extreme that they name: `doc_ids`: document numbers never fall along a micro-batch; a document has at most 1536 tokens.
All inputs are finite; a program needn't handle non-finite values.
Results may differ from the reference program's by a relative error of at most 0.02.
Values may be sent and summed in bfloat16 or wider, within the bound.
No kernel may reach another device: no remote copies, remote signals or barrier semaphores. Data moves between devices by JAX's collectives and lax.ppermute only.
A program may use at most 192 MiB of HBM per device.

```python
import math
import jax
import jax.numpy as jnp
import numpy as np
from jax import lax

D = 8192
HL = 8
HD = 128
TOK_DEV = 512
HEADS = 32
SECTIONS = 2
TOKENS = 2048
WINDOW = 512
DOCS = 2


def paired_parts(key):
    shape = (SECTIONS, TOKENS // 2, 2, HEADS, HD)
    base = jnp.clip(jax.random.normal(jax.random.fold_in(key, 11), shape, jnp.float32), -4.0, 4.0)
    second = jnp.clip(jax.random.normal(jax.random.fold_in(key, 12), shape, jnp.float32), -4.0, 4.0)
    return (base, second)


def draw_queries(key, part):
    base, second = paired_parts(key)
    result = base
    return result.reshape(SECTIONS, TOKENS, HEADS * HD).astype(jnp.bfloat16)


def draw_keys(key, part):
    base, second = paired_parts(key)
    result = second
    return result.reshape(SECTIONS, TOKENS, HEADS * HD).astype(jnp.bfloat16)


def block_levels(stream_key, dims, shards, low, largest):
    def one(dim, parts):
        heights = jax.random.uniform(jax.random.fold_in(jax.random.fold_in(stream_key, 6), dim), (parts,), jnp.float32, low / len(shards), largest / len(shards))
        return jnp.repeat(jnp.exp(heights), dims[dim] // parts).reshape((-1,) + (1,) * (len(dims) - dim - 1))

    gain = one(*shards[0])
    for cut in shards[1:]:
        gain = gain * one(*cut)
    return gain


def split_up(count, total, bound, slope):
    loads = [(1 << 20) // math.isqrt(grade ** slope) + 1 for grade in range(2, count + 1)]
    rest, given = total - bound - (count - 1), [1] * (count - 1)
    while rest > 0:
        movable = [i for i in range(count - 1) if given[i] < bound]
        mass, remaining = sum([loads[i] for i in movable]), rest
        for i in movable:
            addition = min(bound - given[i], max(1, remaining * loads[i] // mass), rest)
            given[i] = given[i] + addition
            rest = rest - addition
    return np.array([bound] + given)


def ragged(rng, count, total, bound, slope):
    if count == 2:
        one = jax.random.randint(rng, (), max(1, total - bound), min(bound, total - 1) + 1)
        return jnp.stack([one, total - one])
    lengths = jnp.asarray(split_up(count, total, bound, slope), jnp.int32)
    couples = (count - 1) // 2
    giver, taker = lengths[1:1 + 2 * couples:2], lengths[2:2 + 2 * couples:2]
    slack = jnp.minimum(giver - 1, bound - taker)
    passed = jax.random.randint(jax.random.fold_in(rng, 1), (couples,), 0, 1 << 20) % (slack + 1)
    lengths = lengths.at[1:1 + 2 * couples:2].set(giver - passed).at[2:2 + 2 * couples:2].set(taker + passed)
    return lengths[jax.random.permutation(jax.random.fold_in(rng, 2), count)]


def bell_draw(key, shape, width, most, split=(), kind=jnp.bfloat16):
    values = jax.random.normal(key, shape, jnp.float32) * width
    if len(split) > 0:
        values = block_levels(key, shape, split, -0.22, 0.18) * values
    return jnp.clip(values, min=-most, max=most).astype(kind)


def setup_inputs(seed: int = 0) -> dict:
    key_of = jax.random.split(jax.random.key(seed), 8)
    return {
        "queries": draw_queries(jax.random.fold_in(key_of[7], 71), 0),
        "keys": draw_keys(jax.random.fold_in(key_of[7], 71), 0),
        "values": bell_draw(key_of[2], (SECTIONS, TOKENS, HEADS * HD), 1.0, 6.0, ((0, 2), (1, 4), (2, 4))),
        "stream": bell_draw(key_of[3], (SECTIONS, TOKENS, D), 1.0, 6.0, ((0, 2), (1, 4), (2, 4))),
        "grad_stream": bell_draw(key_of[4], (SECTIONS, TOKENS, D), 1.0, 6.0, ((0, 2), (1, 4), (2, 4))),
        "out_proj": bell_draw(key_of[5], (SECTIONS, HEADS * HD, D), (HEADS * HD) ** -0.5, 0.09375, ((0, 2), (1, 4))),
        "doc_ids": jax.vmap(lambda own: jnp.searchsorted(jnp.cumsum(ragged(own, DOCS, TOKENS, 3 * TOK_DEV, 0)), jnp.arange(TOKENS), side="right"))(jax.random.split(key_of[6], SECTIONS)).reshape((SECTIONS, TOKENS)).astype(jnp.int32),
    }


NEG = -1.0e30


def block_terms(query_block, key_block, value_block, dout_block, visible):
    scaling = HD ** -0.5
    query_wide = query_block.astype(jnp.float32)
    key_wide = key_block.astype(jnp.float32)
    value_wide = value_block.astype(jnp.float32)
    dout_wide = dout_block.astype(jnp.float32)
    scores = jnp.einsum("qhd,khd->hqk", query_wide, key_wide) * scaling
    masked = jnp.where(visible[None], scores, NEG)
    row_max = jnp.max(masked, axis=-1, keepdims=True)
    exponent = jnp.where(visible[None], jnp.exp(masked - row_max), 0.0)
    row_sum = jnp.sum(exponent, axis=-1, keepdims=True)
    probability = exponent / row_sum
    weights = probability.astype(jnp.bfloat16)
    weights_wide = weights.astype(jnp.float32)
    attended = jnp.einsum("hqk,khd->qhd", weights_wide, value_wide).astype(jnp.bfloat16)
    row_delta = jnp.einsum("qhd,qhd->hq", dout_wide, attended.astype(jnp.float32))[..., None]
    d_prob = jnp.einsum("qhd,khd->hqk", dout_wide, value_wide)
    d_score = (probability * (d_prob - row_delta)).astype(jnp.bfloat16).astype(jnp.float32)
    d_value = jnp.einsum("hqk,qhd->khd", weights_wide, dout_wide)
    d_query = (jnp.einsum("hqk,khd->qhd", d_score, key_wide) * scaling).astype(jnp.bfloat16)
    d_key = jnp.einsum("hqk,qhd->khd", d_score, query_wide) * scaling
    return attended, d_query, d_key, d_value


def one_section(queries, keys, values, stream, grad_stream, out_proj, doc_ids):
    blocks = TOKENS // TOK_DEV
    feature = queries.shape[1]
    head_count = feature // HD
    d_out = lax.dot_general(grad_stream, out_proj, (((1,), (1,)), ((), ())), preferred_element_type=jnp.float32).astype(jnp.bfloat16)

    def to_blocks(array):
        return array.reshape(blocks, TOK_DEV, head_count, HD)

    zero_block = jnp.zeros((1, TOK_DEV, head_count, HD), jnp.bfloat16)
    key_pad = jnp.concatenate([zero_block, to_blocks(keys)], 0)
    value_pad = jnp.concatenate([zero_block, to_blocks(values)], 0)
    key_pairs = jnp.concatenate([key_pad[:-1], key_pad[1:]], 1)
    value_pairs = jnp.concatenate([value_pad[:-1], value_pad[1:]], 1)
    doc_blocks = doc_ids.reshape(blocks, TOK_DEV).astype(jnp.int32)
    doc_pad = jnp.concatenate([jnp.full((1, TOK_DEV), -1, jnp.int32), doc_blocks], 0)
    key_docs = jnp.concatenate([doc_pad[:-1], doc_pad[1:]], 1)
    block_index = jnp.arange(blocks, dtype=jnp.int32)

    def block_step(block_item):
        query_block, key_block, value_block, dout_block, query_doc, key_doc, position = block_item
        query_pos = position * TOK_DEV + jnp.arange(TOK_DEV, dtype=jnp.int32)
        key_pos = (position - 1) * TOK_DEV + jnp.arange(2 * TOK_DEV, dtype=jnp.int32)
        visible = (key_pos[None, :] <= query_pos[:, None]) & (query_pos[:, None] - key_pos[None, :] < WINDOW)
        visible = visible & (key_pos[None, :] >= 0) & (key_doc[None, :] == query_doc[:, None])
        return block_terms(query_block, key_block, value_block, dout_block, visible)

    attended, d_query, d_key, d_value = lax.map(block_step, (to_blocks(queries), key_pairs, value_pairs, to_blocks(d_out), doc_blocks, key_docs, block_index))
    attended_all = attended.reshape(TOKENS, feature)
    group_width = HL * HD
    groups = feature // group_width
    branch = jnp.zeros((TOKENS, out_proj.shape[1]), jnp.float32)
    for group in range(groups):
        part = jnp.dot(attended_all[:, group * group_width:(group + 1) * group_width], out_proj[group * group_width:(group + 1) * group_width], preferred_element_type=jnp.float32).astype(jnp.bfloat16)
        part = lax.optimization_barrier(part)
        branch = branch + part.astype(jnp.float32)
    rebuilt = (stream.astype(jnp.float32) - branch).astype(jnp.bfloat16)
    zero_terms = jnp.zeros((1, TOK_DEV, head_count, HD), jnp.float32)
    key_total = d_key[:, TOK_DEV:] + jnp.concatenate([d_key[1:, :TOK_DEV], zero_terms], 0)
    value_total = d_value[:, TOK_DEV:] + jnp.concatenate([d_value[1:, :TOK_DEV], zero_terms], 0)
    grad_queries = d_query.reshape(TOKENS, feature)
    grad_keys = key_total.astype(jnp.bfloat16).reshape(TOKENS, feature)
    grad_values = value_total.astype(jnp.bfloat16).reshape(TOKENS, feature)
    return grad_queries, grad_keys, grad_values, rebuilt


def reference(queries, keys, values, stream, grad_stream, out_proj, doc_ids):
    results = []
    for section_index in range(SECTIONS):
        results.append(one_section(queries[section_index], keys[section_index], values[section_index], stream[section_index], grad_stream[section_index], out_proj[section_index], doc_ids[section_index]))
    grad_queries = jnp.stack([item[0] for item in results])
    grad_keys = jnp.stack([item[1] for item in results])
    grad_values = jnp.stack([item[2] for item in results])
    next_stream = jnp.stack([results[(section_index + 1) % SECTIONS][3] for section_index in range(SECTIONS)])
    next_grad = jnp.stack([grad_stream[(section_index + 1) % SECTIONS] for section_index in range(SECTIONS)])
    return (grad_queries, grad_keys, grad_values, next_stream, next_grad)
```

```python
import functools

import jax
import jax.numpy as jnp
from jax import lax
from jax.experimental import pallas as pl
from jax.experimental.pallas import tpu as pltpu
from jax.sharding import PartitionSpec as P

HD = 128
WINDOW = 512
NEG = -1e30
HALF = 256
VMEM_LIMIT = 48 * 1024 * 1024

OUTER = [(0, 1), (1, 0), (2, 3), (3, 2)]
MIDDLE = [(1, 2), (2, 1)]
OUTER_INWARD = [(0, 1), (3, 2)]
OUTER_OUTWARD = [(1, 0), (2, 3)]


def params():
    return pltpu.CompilerParams(vmem_limit_bytes=VMEM_LIMIT)


def dot(a, b, contract):
    return lax.dot_general(a, b, ((contract[0], contract[1]), ((), ())), preferred_element_type=jnp.float32)


def nt(a, b):
    return dot(a, b, ((1,), (1,)))


def nn(a, b):
    return dot(a, b, ((1,), (0,)))


def tn(a, b):
    return dot(a, b, ((0,), (0,)))


def lower(size):
    row = lax.broadcasted_iota(jnp.int32, (size, size), 0)
    col = lax.broadcasted_iota(jnp.int32, (size, size), 1)
    return col <= row


def forward_kernel(index_ref, doc_ref, q_ref, k_ref, v_ref, kp_ref, vp_ref, att_ref, w_ref, bias_ref):
    rows = q_ref.shape[0]
    scaling = HD ** (-0.5)

    @pl.when(pl.program_id(0) == 0)
    def _():
        index = index_ref[0]
        own = doc_ref[:, pl.ds(pl.multiple_of(index * rows, rows), rows)]
        before = doc_ref[:, pl.ds(pl.multiple_of(jnp.maximum(index - 1, 0) * rows, rows), rows)]
        before = jnp.where(index > 0, before, -1)
        own = jnp.broadcast_to(own, (rows, rows))
        before = jnp.broadcast_to(before, (rows, rows))
        key_doc = jnp.where(lower(rows), own, before)
        bias_ref[...] = jnp.where(key_doc == own.T, 0.0, NEG)

    tri = lower(HALF)
    for qb in range(2):
        qs = pl.ds(qb * HALF, HALF)
        ks = pl.ds((1 - qb) * HALF, HALF)
        q = q_ref[qs, :]
        diagonal = jnp.where(tri, nt(q, k_ref[qs, :]), nt(q, kp_ref[qs, :]))
        if qb == 0:
            other = nt(q, kp_ref[ks, :])
            scores = jnp.concatenate([diagonal, other], 1)
        else:
            other = nt(q, k_ref[ks, :])
            scores = jnp.concatenate([other, diagonal], 1)
        scores = scores * scaling + bias_ref[qs, :]
        row_max = jnp.max(scores, axis=1, keepdims=True)
        exponent = jnp.exp(scores - row_max)
        row_sum = jnp.sum(exponent, axis=1, keepdims=True)
        prob = exponent * (1.0 / row_sum)
        w_ref[0, qs, :] = prob.astype(jnp.bfloat16)
        mine = prob[:, qb * HALF : (qb + 1) * HALF]
        rest = prob[:, (1 - qb) * HALF : (2 - qb) * HALF].astype(jnp.bfloat16)
        mine_own = jnp.where(tri, mine, 0.0).astype(jnp.bfloat16)
        mine_before = jnp.where(tri, 0.0, mine).astype(jnp.bfloat16)
        att = nn(mine_own, v_ref[qs, :]) + nn(mine_before, vp_ref[qs, :])
        att = att + nn(rest, (vp_ref if qb == 0 else v_ref)[ks, :])
        att_ref[qs, :] = att.astype(jnp.bfloat16)


def forward(index, doc, q, k, v, kp, vp):
    rows, feature = q.shape
    heads = feature // HD
    head = pl.BlockSpec((rows, HD), lambda h, *_: (0, h))
    return pl.pallas_call(
        forward_kernel,
        grid_spec=pltpu.PrefetchScalarGridSpec(
            num_scalar_prefetch=1,
            grid=(heads,),
            in_specs=[pl.BlockSpec(doc.shape, lambda h, *_: (0, 0))] + [head] * 5,
            out_specs=[head, pl.BlockSpec((1, rows, rows), lambda h, *_: (h, 0, 0))],
            scratch_shapes=[pltpu.VMEM((rows, rows), jnp.float32)],
        ),
        out_shape=[
            jax.ShapeDtypeStruct((rows, feature), jnp.bfloat16),
            jax.ShapeDtypeStruct((heads, rows, rows), jnp.bfloat16),
        ],
        compiler_params=params(),
        cost_estimate=pl.CostEstimate(flops=12 * 2 * 2**23 * heads, bytes_accessed=2**23, transcendentals=rows * rows * heads),
        name="attend",
    )(index, doc, q, k, v, kp, vp)


def project_kernel(counts, has_total, index_ref, *refs):
    w_refs = refs[: len(counts)]
    refs = refs[len(counts) :]
    out_ref = refs[-1]
    total = refs[-2][...] if has_total else None
    at = 0
    for w_ref, count in zip(w_refs, counts):
        x = refs[at][...]
        for other in refs[at + 1 : at + count]:
            x = x + other[...]
        at += count
        term = nt(x, w_ref[...])
        total = term if total is None else total + term
    out_ref[...] = total


def project(weight, index, groups, total, chunk):
    rows = HALF
    depth = groups[0][0].shape[1]
    heads_rows = weight.shape[0]
    block = 256
    counts = tuple(len(g) for g in groups)
    w_specs = [pl.BlockSpec((block, depth), lambda n, idx, j=j: (n, idx[j])) for j in range(len(groups))]
    flat, specs = [], []
    for g in groups:
        for x in g:
            flat.append(x)
            at = chunk if x.shape[0] > rows else 0
            specs.append(pl.BlockSpec((rows, depth), lambda n, idx, at=at: (at, 0)))
    if total is not None:
        flat.append(total)
        specs.append(pl.BlockSpec((rows, block), lambda n, idx: (0, n)))
    return pl.pallas_call(
        functools.partial(project_kernel, counts, total is not None),
        grid_spec=pltpu.PrefetchScalarGridSpec(
            num_scalar_prefetch=1,
            grid=(heads_rows // block,),
            in_specs=w_specs + specs,
            out_specs=pl.BlockSpec((rows, block), lambda n, idx: (0, n)),
        ),
        out_shape=jax.ShapeDtypeStruct((rows, heads_rows), jnp.float32),
        compiler_params=params(),
        cost_estimate=pl.CostEstimate(flops=2 * rows * depth * heads_rows * len(groups), bytes_accessed=4 * 2**20 * len(groups), transcendentals=0),
        name="project",
    )(index, *([weight] * len(groups)), *flat)


def part_kernel(received, has_stream, index_ref, x_ref, w_ref, *refs):
    out_ref = refs[-1]
    total = nn(x_ref[...], w_ref[...])
    for ref in refs[:received]:
        total = total + ref[...].astype(jnp.float32)
    if has_stream:
        total = refs[received][...].astype(jnp.float32) - total
    out_ref[...] = total.astype(jnp.bfloat16)


def part(weight, index, attended, received, stream, start, rows):
    depth = weight.shape[0]
    width = stream.shape[1] if stream is not None else weight.shape[1] // 4
    block = 512
    steps = width // block
    at = start // rows
    extra = []
    specs = []
    for x in received:
        extra.append(x)
        specs.append(pl.BlockSpec((rows, block), lambda n, idx: (0, n)))
    if stream is not None:
        extra.append(stream)
        specs.append(pl.BlockSpec((rows, block), lambda n, idx: (at, n)))
    return pl.pallas_call(
        functools.partial(part_kernel, len(received), stream is not None),
        grid_spec=pltpu.PrefetchScalarGridSpec(
            num_scalar_prefetch=1,
            grid=(steps,),
            in_specs=[
                pl.BlockSpec((rows, depth), lambda n, idx: (at, 0)),
                pl.BlockSpec((depth, block), lambda n, idx: (0, idx[0] * steps + n)),
            ]
            + specs,
            out_specs=pl.BlockSpec((rows, block), lambda n, idx: (0, n)),
        ),
        out_shape=jax.ShapeDtypeStruct((rows, width), jnp.bfloat16),
        compiler_params=params(),
        cost_estimate=pl.CostEstimate(flops=2 * rows * depth * width, bytes_accessed=6 * 2**20, transcendentals=0),
        name="part",
    )(index, attended, weight, *extra)


def backward_kernel(qb, index_ref, w_ref, total_ref, x_ref, y_ref, p_ref, att_ref, q_ref, k_ref, v_ref, kp_ref, vp_ref, *refs):
    scaling = HD ** (-0.5)
    qs = pl.ds(qb * HALF, HALF)
    ks = pl.ds((1 - qb) * HALF, HALF)
    tri = lower(HALF)
    bf = jnp.bfloat16
    d_out = (total_ref[...] + nt(x_ref[...] + y_ref[...], w_ref[...])).astype(bf)
    row_delta = jnp.sum(d_out.astype(jnp.float32) * att_ref[...].astype(jnp.float32), axis=1, keepdims=True)
    q = q_ref[...]
    k_diag, kp_diag = k_ref[qs, :], kp_ref[qs, :]
    k_rest, v_rest = ((kp_ref, vp_ref) if qb == 0 else (k_ref, v_ref))
    k_rest, v_rest = k_rest[ks, :], v_rest[ks, :]
    p_diag = p_ref[0, :, qb * HALF : (qb + 1) * HALF].astype(jnp.float32)
    p_rest = p_ref[0, :, (1 - qb) * HALF : (2 - qb) * HALF]
    dp_diag = jnp.where(tri, nt(d_out, v_ref[qs, :]), nt(d_out, vp_ref[qs, :]))
    dp_rest = nt(d_out, v_rest)
    ds_diag = p_diag * (dp_diag - row_delta)
    ds_rest = (p_rest.astype(jnp.float32) * (dp_rest - row_delta)).astype(bf)
    ds_own = jnp.where(tri, ds_diag, 0.0).astype(bf)
    ds_before = jnp.where(tri, 0.0, ds_diag).astype(bf)
    p_own = jnp.where(tri, p_diag, 0.0).astype(bf)
    p_before = jnp.where(tri, 0.0, p_diag).astype(bf)
    dq = nn(ds_own, k_diag) + nn(ds_before, kp_diag) + nn(ds_rest, k_rest)
    dk_own, dv_own = tn(ds_own, q) * scaling, tn(p_own, d_out)
    dk_before, dv_before = tn(ds_before, q) * scaling, tn(p_before, d_out)
    dk_rest, dv_rest = tn(ds_rest, q) * scaling, tn(p_rest, d_out)
    if qb == 0:
        dq_ref, dkb_ref, dvb_ref, dk0_ref, dv0_ref, dkr_ref, dvr_ref = refs
        dkb_ref[...] = dk_before.astype(bf)
        dvb_ref[...] = dv_before.astype(bf)
        dk0_ref[...] = dk_own
        dv0_ref[...] = dv_own
        dkr_ref[...] = dk_rest
        dvr_ref[...] = dv_rest
    else:
        dk0i, dv0i, dkri, dvri, dq_ref, dkb_ref, dvb_ref, dk0_ref, dv0_ref, dk1_ref, dv1_ref = refs
        dkb_ref[...] = (dk_before + dkri[...]).astype(bf)
        dvb_ref[...] = (dv_before + dvri[...]).astype(bf)
        dk0_ref[...] = dk_rest + dk0i[...]
        dv0_ref[...] = dv_rest + dv0i[...]
        dk1_ref[...] = dk_own
        dv1_ref[...] = dv_own
    dq_ref[...] = (dq * scaling).astype(bf)


def backward(qb, weight, index, total, x, y, probs, attended, q, k, v, kp, vp, carried):
    rows, feature = q.shape
    heads = feature // HD
    depth = x.shape[1]
    x_at = qb if x.shape[0] > HALF else 0
    y_at = qb if y.shape[0] > HALF else 0
    head = pl.BlockSpec((rows, HD), lambda h, *_: (0, h))
    half = pl.BlockSpec((HALF, HD), lambda h, *_: (0, h))
    mine = pl.BlockSpec((HALF, HD), lambda h, *_: (qb, h))
    bf16_out = jax.ShapeDtypeStruct((HALF, feature), jnp.bfloat16)
    f32_out = jax.ShapeDtypeStruct((HALF, feature), jnp.float32)
    return pl.pallas_call(
        functools.partial(backward_kernel, qb),
        grid_spec=pltpu.PrefetchScalarGridSpec(
            num_scalar_prefetch=1,
            grid=(heads,),
            in_specs=[
                pl.BlockSpec((HD, depth), lambda h, idx: (h, idx[0])),
                half,
                pl.BlockSpec((HALF, depth), lambda h, *_: (x_at, 0)),
                pl.BlockSpec((HALF, depth), lambda h, *_: (y_at, 0)),
                pl.BlockSpec((1, HALF, rows), lambda h, *_: (h, qb, 0)),
                mine,
                mine,
                head,
                head,
                head,
                head,
            ]
            + [half] * len(carried),
            out_specs=[half] * 7,
        ),
        out_shape=[bf16_out] * 3 + [f32_out] * 4,
        compiler_params=params(),
        cost_estimate=pl.CostEstimate(flops=2 * HALF * depth * feature * 3, bytes_accessed=16 * 2**20, transcendentals=0),
        name="backward",
    )(index, weight, total, x, y, probs, attended, q, k, v, kp, vp, *carried)


def from_behind(block, axis, distance):
    devices = range(lax.axis_size(axis))
    route = [(i - distance, i) for i in devices if i - distance in devices]
    return lax.ppermute(block, axis, route)


def shifted(block, axis, distance):
    count = lax.axis_size(axis)
    return lax.ppermute(block, axis, [((i - distance) % count, i) for i in range(count)])


def hop(block, pairs):
    return lax.ppermute(block, "tp", pairs)


def body(queries, keys, values, stream, grad_stream, out_proj, doc_ids):
    q, k, v, weight = queries[0], keys[0], values[0], out_proj[0]
    grad = grad_stream[0]
    rows, feature = q.shape
    chunks = rows // HALF
    me = lax.axis_index("tp").astype(jnp.int32)
    ctx = lax.axis_index("ctx").astype(jnp.int32)
    near, across, far = me ^ 1, me ^ 2, 3 - me
    one = lambda x: x.reshape(1)

    kp = from_behind(k, "ctx", 1)
    vp = from_behind(v, "ctx", 1)
    pieces = [grad[c * HALF : (c + 1) * HALF] for c in range(chunks)]
    o1 = [hop(x, OUTER) for x in pieces]
    m1 = [hop(x, MIDDLE) for x in pieces]
    grad_next = shifted(grad_stream, "pipe", -1)
    attended, probs = forward(one(ctx), doc_ids, q, k, v, kp, vp)
    m2 = [hop(x, MIDDLE) for x in o1]
    i2 = [hop(x, OUTER_OUTWARD) for x in m1]
    i3 = [hop(x, OUTER_OUTWARD) for x in m2]

    sa = [part(weight, one(far), attended, [], None, c * HALF, HALF) for c in range(chunks)]
    e2 = [hop(x, OUTER_INWARD) for x in sa]
    sb = [part(weight, one(across), attended, [e2[c]], None, c * HALF, HALF) for c in range(chunks)]
    n3 = [hop(x, MIDDLE) for x in sb]
    e3 = [hop(x, OUTER_INWARD) for x in sb]
    sc = [part(weight, one(near), attended, [n3[c]], None, c * HALF, HALF) for c in range(chunks)]
    sd = [part(weight, one(far), attended, [e3[c]], None, c * HALF, HALF) for c in range(chunks)]
    f4 = [hop(x, OUTER) for x in sc]
    n4 = [hop(x, MIDDLE) for x in sd]
    rebuilt = [
        part(weight, one(me), attended, [f4[c], n4[c]], stream[0], c * HALF, HALF) for c in range(chunks)
    ]
    stream_next = jnp.concatenate([shifted(x, "pipe", -1) for x in rebuilt], 0)[None]

    totals = [project(weight, jnp.stack([me, near]), [[grad], [o1[c]]], None, c) for c in range(chunks)]
    totals = [project(weight, one(across), [[m2[c], i2[c]]], totals[c], c) for c in range(chunks)]
    first = backward(0, weight, one(far), totals[0], m1[0], i3[0], probs, attended, q, k, v, kp, vp, ())
    dq0, dkb0, dvb0, dk0, dv0, dkr, dvr = first
    ret_k0, ret_v0 = from_behind(dkb0, "ctx", -1), from_behind(dvb0, "ctx", -1)
    second = backward(1, weight, one(far), totals[1], m1[1], i3[1], probs, attended, q, k, v, kp, vp, (dk0, dv0, dkr, dvr))
    dq1, dkb1, dvb1, dk0, dv0, dk1, dv1 = second
    ret_k1, ret_v1 = from_behind(dkb1, "ctx", -1), from_behind(dvb1, "ctx", -1)

    def finish(a0, a1, r0, r1):
        return jnp.concatenate([(a0 + r0).astype(jnp.bfloat16), (a1 + r1).astype(jnp.bfloat16)], 0)[None]

    grad_queries = jnp.concatenate([dq0, dq1], 0)[None]
    grad_keys = finish(dk0, dk1, ret_k0, ret_k1)
    grad_values = finish(dv0, dv1, ret_v0, ret_v1)
    return (grad_queries, grad_keys, grad_values, stream_next, grad_next)


def solution(mesh):
    cut = P("pipe", "ctx", "tp")
    in_specs = (cut, cut, cut, cut, cut, P("pipe", "tp", None), P("pipe", None))
    out_specs = (cut, cut, cut, cut, cut)
    return jax.shard_map(body, mesh=mesh, in_specs=in_specs, out_specs=out_specs, check_vma=False)
```

```python
import functools

import jax
import jax.numpy as jnp
from jax import lax
from jax.experimental import pallas as pl
from jax.experimental.pallas import tpu as pltpu
from jax.sharding import PartitionSpec as P

HD = 128
WINDOW = 512
NEG = -1e30
HALF = 256
PIECES = [(0, 256), (256, 128), (384, 128)]
PAIR = 2
VMEM_LIMIT = 50 * 1024 * 1024
COST = 1.0

OUTER = [(0, 1), (1, 0), (2, 3), (3, 2)]
MIDDLE = [(1, 2), (2, 1)]
OUTER_INWARD = [(0, 1), (3, 2)]
OUTER_OUTWARD = [(1, 0), (2, 3)]


def params():
    return pltpu.CompilerParams(vmem_limit_bytes=VMEM_LIMIT)


def dot(a, b, contract):
    return lax.dot_general(a, b, ((contract[0], contract[1]), ((), ())), preferred_element_type=jnp.float32)


def nt(a, b):
    return dot(a, b, ((1,), (1,)))


def nn(a, b):
    return dot(a, b, ((1,), (0,)))


def tn(a, b):
    return dot(a, b, ((0,), (0,)))


def lower(size):
    row = lax.broadcasted_iota(jnp.int32, (size, size), 0)
    col = lax.broadcasted_iota(jnp.int32, (size, size), 1)
    return col <= row


def forward_kernel(index_ref, doc_ref, q_ref, k_ref, v_ref, kp_ref, vp_ref, att_ref, w_ref, bias_ref):
    rows = q_ref.shape[0]
    scaling = HD ** (-0.5)

    @pl.when(pl.program_id(0) == 0)
    def _():
        index = index_ref[0]
        own = doc_ref[:, pl.ds(pl.multiple_of(index * rows, rows), rows)]
        before = doc_ref[:, pl.ds(pl.multiple_of(jnp.maximum(index - 1, 0) * rows, rows), rows)]
        before = jnp.where(index > 0, before, -1)
        own = jnp.broadcast_to(own, (rows, rows))
        before = jnp.broadcast_to(before, (rows, rows))
        key_doc = jnp.where(lower(rows), own, before)
        bias_ref[...] = jnp.where(key_doc == own.T, 0.0, NEG)

    tri = lower(HALF)
    for head in range(q_ref.shape[1] // HD):
        cols = pl.ds(head * HD, HD)
        for qb in range(2):
            qs = pl.ds(qb * HALF, HALF)
            ks = pl.ds((1 - qb) * HALF, HALF)
            q = q_ref[qs, cols]
            diagonal = jnp.where(tri, nt(q, k_ref[qs, cols]), nt(q, kp_ref[qs, cols]))
            if qb == 0:
                scores = jnp.concatenate([diagonal, nt(q, kp_ref[ks, cols])], 1)
            else:
                scores = jnp.concatenate([nt(q, k_ref[ks, cols]), diagonal], 1)
            scores = scores * scaling + bias_ref[qs, :]
            row_max = jnp.max(scores, axis=1, keepdims=True)
            exponent = jnp.exp(scores - row_max)
            row_sum = jnp.sum(exponent, axis=1, keepdims=True)
            prob = exponent * (1.0 / row_sum)
            w_ref[head, qs, :] = prob.astype(jnp.bfloat16)
            mine = prob[:, qb * HALF : (qb + 1) * HALF]
            rest = prob[:, (1 - qb) * HALF : (2 - qb) * HALF].astype(jnp.bfloat16)
            mine_own = jnp.where(tri, mine, 0.0).astype(jnp.bfloat16)
            mine_before = jnp.where(tri, 0.0, mine).astype(jnp.bfloat16)
            att = nn(mine_own, v_ref[qs, cols]) + nn(mine_before, vp_ref[qs, cols])
            att = att + nn(rest, (vp_ref if qb == 0 else v_ref)[ks, cols])
            att_ref[qs, cols] = att.astype(jnp.bfloat16)


def cost(flops, moved, transcendentals=0):
    return pl.CostEstimate(flops=int(flops * COST), bytes_accessed=int(moved * COST), transcendentals=int(transcendentals * COST))


ANY = pl.BlockSpec(memory_space=pl.ANY)


def call(kernel, index, grid, blocked, after, out_specs, out_shape, moved, flops, name, scratch=(), aliases=None):
    count = len(blocked)
    waits = len(after)
    outs = len(out_shape)

    def run(index_ref, *refs):
        kernel(index_ref, *refs[:count], *refs[count + waits : count + waits + outs], *refs[count + waits + outs + 1 :])
        refs[count + waits + outs][0, 0] = jnp.float32(0.0)

    result = pl.pallas_call(
        run,
        grid_spec=pltpu.PrefetchScalarGridSpec(
            num_scalar_prefetch=1,
            grid=grid,
            in_specs=[spec for _, spec in blocked] + [ANY] * waits,
            out_specs=list(out_specs) + [pl.BlockSpec((1, 1), lambda *_: (0, 0), memory_space=pltpu.SMEM)],
            scratch_shapes=list(scratch),
        ),
        out_shape=list(out_shape) + [jax.ShapeDtypeStruct((1, 1), jnp.float32)],
        input_output_aliases=aliases or {},
        compiler_params=params(),
        cost_estimate=cost(flops, moved),
        name=name,
    )(index, *[x for x, _ in blocked], *after)
    return result[:-1], result[-1].reshape(())


def tie(index, after):
    _, zero = call(lambda index_ref: None, index, (1,), [], after, [], [], 8192, 0, "tie")
    return zero


def forward(index, doc, q, k, v, kp, vp):
    rows, feature = q.shape
    heads = feature // HD
    head = pl.BlockSpec((rows, PAIR * HD), lambda h, *_: (0, h))
    return call(
        forward_kernel, index, (heads // PAIR,),
        [(doc, pl.BlockSpec(doc.shape, lambda h, *_: (0, 0)))] + [(x, head) for x in (q, k, v, kp, vp)], [],
        [head, pl.BlockSpec((PAIR, rows, rows), lambda h, *_: (h, 0, 0))],
        [jax.ShapeDtypeStruct((rows, feature), jnp.bfloat16), jax.ShapeDtypeStruct((heads, rows, rows), jnp.bfloat16)],
        2**23, 12 * 2 * 2**23 * heads, "attend", scratch=[pltpu.VMEM((rows, rows), jnp.float32)],
    )


def project(weight, index, groups, total, after):
    rows = sum(piece[0].shape[0] for piece in groups[0])
    depth = groups[0][0][0].shape[1]
    out_rows = weight.shape[0]
    block = 256
    shape = [[(len(piece), piece[0].shape[0]) for piece in g] for g in groups]
    has_total = total is not None

    def kernel(index_ref, *refs):
        refs = list(refs)
        w = [refs.pop(0)[...] for _ in groups]
        out_ref = refs[-1]
        start = 0
        base = refs[-2] if has_total else None
        sums = {}
        for j, pieces in enumerate(shape):
            start = 0
            for many, height in pieces:
                x = refs.pop(0)[...]
                for _ in range(many - 1):
                    x = x + refs.pop(0)[...]
                term = nt(x, w[j])
                key = (start, height)
                at = pl.ds(start, height)
                if j == 0:
                    out_ref[at, :] = term + base[at, :] if has_total else term
                else:
                    out_ref[at, :] += term
                start += height

    blocked = [(weight, pl.BlockSpec((block, depth), lambda n, idx, j=j: (n, idx[j]))) for j in range(len(groups))]
    for g in groups:
        for piece in g:
            for x in piece:
                blocked.append((x, pl.BlockSpec(x.shape, lambda n, idx: (0, 0))))
    if has_total:
        blocked.append((total, pl.BlockSpec((rows, block), lambda n, idx: (0, n))))
    return call(
        kernel, index, (out_rows // block,), blocked, after,
        [pl.BlockSpec((rows, block), lambda n, idx: (0, n))],
        [jax.ShapeDtypeStruct((rows, out_rows), jnp.float32)],
        2 * out_rows * depth * len(groups), 2 * rows * depth * out_rows * len(groups), "project",
    )


def parts(weight, index, attended, count, after, stream=None):
    rows, depth = attended.shape
    width = weight.shape[1] // 4
    block = 512
    steps = width // block

    def kernel(index_ref, x_ref, *refs):
        base = count + (stream is not None)
        for j in range(count):
            out = nn(x_ref[...], refs[j][...])
            if stream is not None and j == count - 1:
                out = refs[count][...].astype(jnp.float32) - out
            out = out.astype(jnp.bfloat16)
            refs[base + 2 * j][...] = out[:HALF]
            refs[base + 2 * j + 1][...] = out[HALF:]

    blocked = [(attended, pl.BlockSpec((rows, depth), lambda n, idx: (0, 0)))]
    for j in range(count):
        blocked.append((weight, pl.BlockSpec((depth, block), lambda n, idx, j=j: (0, idx[j] * steps + n))))
    if stream is not None:
        blocked.append((stream, pl.BlockSpec((rows, block), lambda n, idx: (0, n))))
    return call(
        kernel, index, (steps,), blocked, after,
        [pl.BlockSpec((HALF, block), lambda n, idx: (0, n))] * (2 * count),
        [jax.ShapeDtypeStruct((HALF, width), jnp.bfloat16)] * (2 * count),
        count * 2 * depth * width, 2 * rows * depth * width * count, "parts",
    )


def place(index, whole, rows, piece, start, after):
    height, width = piece.shape
    extra = list(after)
    aliases = None
    if whole is not None:
        extra = [whole] + extra
        aliases = {2: 0}

    def kernel(index_ref, x_ref, out_ref):
        out_ref[...] = x_ref[...]

    (out,), zero = call(
        kernel, index, (1,), [(piece, pl.BlockSpec((height, width), lambda n, idx: (0, 0)))], extra,
        [pl.BlockSpec((height, width), lambda n, idx: (start // height, 0))],
        [jax.ShapeDtypeStruct((rows, width), piece.dtype)],
        4 * height * width, 0, "place", aliases=aliases,
    )
    return out, zero


def settle(index, grad_keys, grad_values, k1, v1, back, after):
    height, width = k1.shape
    rows = grad_keys.shape[0]
    wide = 512

    def kernel(index_ref, k_ref, v_ref, back_ref, *refs):
        gk_ref, gv_ref = refs[-2:]
        gk_ref[...] = (k_ref[...] + back_ref[0].astype(jnp.float32)).astype(jnp.bfloat16)
        gv_ref[...] = (v_ref[...] + back_ref[1].astype(jnp.float32)).astype(jnp.bfloat16)

    flat = pl.BlockSpec((height, wide), lambda n, idx: (0, n))
    late = pl.BlockSpec((height, wide), lambda n, idx: (rows // height - 1, n))
    out = jax.ShapeDtypeStruct((rows, width), jnp.bfloat16)
    return call(
        kernel, index, (width // wide,),
        [(k1, flat), (v1, flat), (back, pl.BlockSpec((2, height, wide), lambda n, idx: (0, 0, n)))],
        [grad_keys, grad_values] + list(after), [late, late], [out, out],
        16 * height * width, 0, "settle", aliases={4: 0, 5: 1},
    )


def total_of(*terms):
    result = terms[0].astype(jnp.float32)
    for x in terms[1:]:
        result = result + x.astype(jnp.float32)
    return result


def backward(qb, weight, index, total, outer, middle, probs, attended, q, k, v, kp, vp, carried, after):
    rows, feature = q.shape
    heads = feature // HD
    depth = outer.shape[1]
    wide = PAIR * HD
    scaling = HD ** (-0.5)
    bf = jnp.bfloat16
    skip = len(after) + (1 if qb else 0)

    def kernel(index_ref, w_ref, total_ref, outer_ref, middle_ref, p_ref, att_ref, q_ref, k_ref, v_ref, kp_ref, vp_ref, *refs):
        refs = refs[skip:]
        carry = refs[:5] if qb else ()
        dq_ref, send_ref, k0_ref, v0_ref, k1_ref, v1_ref, x_ref = refs[len(carry) :]

        @pl.when((pl.program_id(0) == 0) & (index_ref[1] == 1))
        def _():
            x_ref[...] = outer_ref[...]

        @pl.when((pl.program_id(0) == 0) & (index_ref[1] == 0))
        def _():
            x_ref[...] = middle_ref[...]

        qs = pl.ds(qb * HALF, HALF)
        ks = pl.ds((1 - qb) * HALF, HALF)
        tri = lower(HALF)
        d_out_pair = (total_ref[...] + nt(x_ref[...], w_ref[...])).astype(bf)
        for head in range(PAIR):
            cols = pl.ds(head * HD, HD)
            d_out = d_out_pair[:, head * HD : (head + 1) * HD]
            row_delta = jnp.sum(
                d_out.astype(jnp.float32) * att_ref[:, cols].astype(jnp.float32), axis=1, keepdims=True
            )
            qh = q_ref[:, cols]
            k_rest_ref, v_rest_ref = (k_ref, v_ref) if qb else (kp_ref, vp_ref)
            k_rest, v_rest = k_rest_ref[ks, cols], v_rest_ref[ks, cols]
            p_diag = p_ref[head, :, qb * HALF : (qb + 1) * HALF].astype(jnp.float32)
            p_rest = p_ref[head, :, (1 - qb) * HALF : (2 - qb) * HALF]
            dp_diag = jnp.where(tri, nt(d_out, v_ref[qs, cols]), nt(d_out, vp_ref[qs, cols]))
            dp_rest = nt(d_out, v_rest)
            ds_diag = p_diag * (dp_diag - row_delta)
            ds_rest = (p_rest.astype(jnp.float32) * (dp_rest - row_delta)).astype(bf)
            ds_own = jnp.where(tri, ds_diag, 0.0).astype(bf)
            ds_before = jnp.where(tri, 0.0, ds_diag).astype(bf)
            p_own = jnp.where(tri, p_diag, 0.0).astype(bf)
            p_before = jnp.where(tri, 0.0, p_diag).astype(bf)
            dq = nn(ds_own, k_ref[qs, cols]) + nn(ds_before, kp_ref[qs, cols]) + nn(ds_rest, k_rest)
            dq_ref[:, cols] = (dq * scaling).astype(bf)
            dk_own, dv_own = tn(ds_own, qh) * scaling, tn(p_own, d_out)
            dk_before, dv_before = tn(ds_before, qh) * scaling, tn(p_before, d_out)
            dk_rest, dv_rest = tn(ds_rest, qh) * scaling, tn(p_rest, d_out)
            if qb == 0:
                send_ref[0, :, cols] = dk_before.astype(bf)
                send_ref[1, :, cols] = dv_before.astype(bf)
                k0_ref[:, cols], v0_ref[:, cols] = dk_own, dv_own
                k1_ref[:, cols], v1_ref[:, cols] = dk_rest, dv_rest
            else:
                k0i, v0i, kri, vri, back = carry
                send_ref[0, :, cols] = (dk_before + kri[:, cols]).astype(bf)
                send_ref[1, :, cols] = (dv_before + vri[:, cols]).astype(bf)
                k0_ref[:, cols] = (dk_rest + k0i[:, cols] + back[0, :, cols].astype(jnp.float32)).astype(bf)
                v0_ref[:, cols] = (dv_rest + v0i[:, cols] + back[1, :, cols].astype(jnp.float32)).astype(bf)
                k1_ref[:, cols], v1_ref[:, cols] = dk_own, dv_own

    whole = pl.BlockSpec((rows, wide), lambda h, *_: (0, h))
    half = pl.BlockSpec((HALF, wide), lambda h, *_: (0, h))
    mine = pl.BlockSpec((HALF, wide), lambda h, *_: (qb, h))
    blocked = [
        (weight, pl.BlockSpec((wide, depth), lambda h, idx: (h, idx[0]))),
        (total, mine),
        (outer, pl.BlockSpec((HALF, depth), lambda h, *_: (0, 0))),
        (middle, pl.BlockSpec((HALF, depth), lambda h, *_: (qb, 0))),
        (probs, pl.BlockSpec((PAIR, HALF, rows), lambda h, *_: (h, qb, 0))),
        (attended, mine),
        (q, mine),
        (k, whole),
        (v, whole),
        (kp, whole),
        (vp, whole),
    ]
    aliases = {}
    extra = list(after)
    if qb:
        extra = [carried[0]] + extra
        aliases = {1 + len(blocked): 0}
    pair = pl.BlockSpec((2, HALF, wide), lambda h, *_: (0, 0, h))
    blocked += [(x, ANY) for x in extra] + [(x, half) for x in carried[1:5]] + [(x, pair) for x in carried[5:]]
    f32_out = jax.ShapeDtypeStruct((HALF, feature), jnp.float32)
    whole_out = jax.ShapeDtypeStruct((rows, feature), bf)
    return call(
        kernel, index, (heads // PAIR,), blocked, [],
        [mine, pair] + [half] * 4,
        [whole_out, jax.ShapeDtypeStruct((2, HALF, feature), bf)] + [whole_out if qb else f32_out] * 2 + [f32_out] * 2,
        16 * 2**20, 2 * HALF * depth * feature * 3, "backward", aliases=aliases,
        scratch=[pltpu.VMEM((HALF, depth), bf)],
    )


def from_behind(block, axis, distance):
    devices = range(lax.axis_size(axis))
    route = [(i - distance, i) for i in devices if i - distance in devices]
    return lax.ppermute(block, axis, route)


def shifted(block, axis, distance):
    count = lax.axis_size(axis)
    return lax.ppermute(block, axis, [((i - distance) % count, i) for i in range(count)])


def hop(block, pairs):
    return lax.ppermute(block, "tp", pairs)


def body(queries, keys, values, stream, grad_stream, out_proj, doc_ids):
    q, k, v, weight = queries[0], keys[0], values[0], out_proj[0]
    grad = grad_stream[0]
    rows, feature = q.shape
    chunks = rows // HALF
    me = lax.axis_index("tp").astype(jnp.int32)
    ctx = lax.axis_index("ctx").astype(jnp.int32)
    near, across, far = me ^ 1, me ^ 2, 3 - me
    one = lambda x: x.reshape(1)

    idx = one(me)
    end = (me == 0) | (me == 3)
    bf = jnp.bfloat16
    half = lambda x, c: x[c * HALF : (c + 1) * HALF]
    both = range(chunks)

    kp = from_behind(k, "ctx", 1)
    vp = from_behind(v, "ctx", 1)
    o1 = hop(grad, OUTER)
    m1 = hop(grad, MIDDLE)
    grad_next = shifted(grad, "pipe", -1)
    (attended, probs), _ = forward(one(ctx), doc_ids, q, k, v, kp, vp)
    pa, zero = parts(weight, one(far), attended, 1, [])
    to_m2, to_x2 = [], []
    for c in both:
        to_x2.append(total_of(jnp.where(end, pa[c], half(m1, c)), zero).astype(bf))
        to_m2.append(total_of(half(o1, c), zero).astype(bf))
        zero = tie(idx, [to_m2[c], to_x2[c]])
    m2 = [hop(x, MIDDLE) for x in to_m2]
    x2 = [hop(x, OUTER) for x in to_x2]
    (pb0, pb1, pc0, pc1, pd0, pd1), _ = parts(weight, jnp.stack([across, near, me]), attended, 3, to_m2 + to_x2, stream[0])
    pb, pc, pd = (pb0, pb1), (pc0, pc1), (pd0, pd1)
    (total,), zero = project(weight, jnp.stack([me, near]), [[(grad,)], [(o1,)]], None, [pb0])
    n3, x3 = [], []
    for c in both:
        to_n3 = total_of(pb[c], x2[c], zero).astype(bf)
        to_x3 = total_of(jnp.where(end, pb[c], m2[c]), zero).astype(bf)
        n3.append(hop(to_n3, MIDDLE))
        x3.append(hop(to_x3, OUTER))
        if c == 0:
            zero = tie(idx, [to_n3, to_x3])
    (total,), zero = project(
        weight, one(across), [[(jnp.where(end, x2[c], m2[c]),) for c in both]], total, [to_n3, to_x3]
    )
    next_grad, zero = place(idx, None, 2 * HALF, grad_next, 0, [total])
    far_and_end = jnp.stack([far, end.astype(jnp.int32)])
    hops = {}

    def launch(p, zero):
        at, height = PIECES[p]
        c = at // HALF
        piece = slice(at - c * HALF, at - c * HALF + height)
        to_f4 = total_of(pc[c][piece], n3[c][piece], zero).astype(bf)
        to_n4 = total_of(pa[c][piece], x3[c][piece], zero).astype(bf)
        hops[p] = (hop(to_f4, OUTER), hop(to_n4, MIDDLE))
        return [to_f4, to_n4]

    arrived, done = [], []

    def finish(p, zero):
        at, height = PIECES[p]
        c = at // HALF
        own = pd[c][at - c * HALF : at - c * HALF + height]
        rebuilt = (own.astype(jnp.float32) - total_of(*hops[p], zero)).astype(bf)
        arrived.append(shifted(rebuilt, "pipe", -1))
        done.append(rebuilt)
        return tie(idx, [rebuilt])

    sends = launch(0, zero)
    (dq, send0, k0, v0, k1, v1), zero = backward(
        0, weight, far_and_end, total, x3[0], m1, probs, attended, q, k, v, kp, vp, (), sends
    )
    back0 = from_behind(send0, "ctx", -1)
    sends = launch(1, zero) + launch(2, zero)
    zero = tie(idx, sends)
    finish(0, zero)
    (dq, send1, grad_keys, grad_values, k1, v1), zero = backward(
        1, weight, far_and_end, total, x3[1], m1, probs, attended, q, k, v, kp, vp, (dq, k0, v0, k1, v1, back0), [done[0]]
    )
    back1 = from_behind(send1, "ctx", -1)
    zero = finish(1, zero)
    finish(2, zero)
    (grad_keys, grad_values), _ = settle(idx, grad_keys, grad_values, k1, v1, back1, [done[2]])
    stream_next, after = None, [grad_keys]
    for (at, height), piece in zip(PIECES, arrived):
        stream_next, _ = place(idx, stream_next, 2 * HALF, piece, at, after)
        after = []
    return tuple(x[None] for x in (dq, grad_keys, grad_values, stream_next, next_grad))


def solution(mesh):
    cut = P("pipe", "ctx", "tp")
    in_specs = (cut, cut, cut, cut, cut, P("pipe", "tp", None), P("pipe", None))
    out_specs = (cut, cut, cut, cut, cut)
    return jax.shard_map(body, mesh=mesh, in_specs=in_specs, out_specs=out_specs, check_vma=False)
```

```python
import functools

import jax
import jax.numpy as jnp
from jax import lax
from jax.experimental import pallas as pl
from jax.experimental.pallas import tpu as pltpu
from jax.sharding import PartitionSpec as P

HD = 128
WINDOW = 512
NEG = -1e30
HALF = 256
PIECES = [(0, 256), (256, 128), (384, 128)]
PAIR = 4
VMEM_LIMIT = 50 * 1024 * 1024
COST = 1.0

OUTER = [(0, 1), (1, 0), (2, 3), (3, 2)]
MIDDLE = [(1, 2), (2, 1)]
OUTER_INWARD = [(0, 1), (3, 2)]
OUTER_OUTWARD = [(1, 0), (2, 3)]


def params():
    return pltpu.CompilerParams(vmem_limit_bytes=VMEM_LIMIT)


def dot(a, b, contract):
    return lax.dot_general(a, b, ((contract[0], contract[1]), ((), ())), preferred_element_type=jnp.float32)


def nt(a, b):
    return dot(a, b, ((1,), (1,)))


def nn(a, b):
    return dot(a, b, ((1,), (0,)))


def tn(a, b):
    return dot(a, b, ((0,), (0,)))


def lower(size):
    row = lax.broadcasted_iota(jnp.int32, (size, size), 0)
    col = lax.broadcasted_iota(jnp.int32, (size, size), 1)
    return col <= row


def forward_kernel(steps, index_ref, doc_ref, q_ref, k_ref, v_ref, kp_ref, vp_ref, far_ref, att_ref, w_ref, far0_ref, far1_ref, bias_ref, all_ref):
    rows = q_ref.shape[0]
    step = pl.program_id(0)
    scaling = HD ** (-0.5)

    @pl.when(step == 0)
    def _():
        index = index_ref[1]
        own = doc_ref[:, pl.ds(pl.multiple_of(index * rows, rows), rows)]
        before = doc_ref[:, pl.ds(pl.multiple_of(jnp.maximum(index - 1, 0) * rows, rows), rows)]
        before = jnp.where(index > 0, before, -1)
        own = jnp.broadcast_to(own, (rows, rows))
        before = jnp.broadcast_to(before, (rows, rows))
        key_doc = jnp.where(lower(rows), own, before)
        bias_ref[...] = jnp.where(key_doc == own.T, 0.0, NEG)

    @pl.when(step < steps)
    def _():
        tri = lower(HALF)
        for head in range(q_ref.shape[1] // HD):
            cols = pl.ds(head * HD, HD)
            for qb in range(2):
                qs = pl.ds(qb * HALF, HALF)
                ks = pl.ds((1 - qb) * HALF, HALF)
                q = q_ref[qs, cols]
                diagonal = jnp.where(tri, nt(q, k_ref[qs, cols]), nt(q, kp_ref[qs, cols]))
                if qb == 0:
                    scores = jnp.concatenate([diagonal, nt(q, kp_ref[ks, cols])], 1)
                else:
                    scores = jnp.concatenate([nt(q, k_ref[ks, cols]), diagonal], 1)
                scores = scores * scaling + bias_ref[qs, :]
                row_max = jnp.max(scores, axis=1, keepdims=True)
                exponent = jnp.exp(scores - row_max)
                row_sum = jnp.sum(exponent, axis=1, keepdims=True)
                prob = exponent * (1.0 / row_sum)
                w_ref[head, qs, :] = prob.astype(jnp.bfloat16)
                mine = prob[:, qb * HALF : (qb + 1) * HALF]
                rest = prob[:, (1 - qb) * HALF : (2 - qb) * HALF].astype(jnp.bfloat16)
                mine_own = jnp.where(tri, mine, 0.0).astype(jnp.bfloat16)
                mine_before = jnp.where(tri, 0.0, mine).astype(jnp.bfloat16)
                att = nn(mine_own, v_ref[qs, cols]) + nn(mine_before, vp_ref[qs, cols])
                att = att + nn(rest, (vp_ref if qb == 0 else v_ref)[ks, cols])
                att_ref[qs, cols] = att.astype(jnp.bfloat16)

    for j in range(steps):

        @pl.when(step == j)
        def _():
            all_ref[j] = att_ref[...]

    @pl.when(step >= steps)
    def _():
        wide = PAIR * HD
        out = nn(all_ref[0], far_ref[:wide, :])
        for j in range(1, steps):
            out += nn(all_ref[j], far_ref[j * wide : (j + 1) * wide, :])
        out = out.astype(jnp.bfloat16)
        far0_ref[...] = out[:HALF]
        far1_ref[...] = out[HALF:]


def cost(flops, moved, transcendentals=0):
    return pl.CostEstimate(flops=int(flops * COST), bytes_accessed=int(moved * COST), transcendentals=int(transcendentals * COST))


ANY = pl.BlockSpec(memory_space=pl.ANY)


def corner(x):
    block = (1,) * (x.ndim - 2) + (16, HD)
    return pl.BlockSpec(block, lambda *_: (0,) * x.ndim)


def call(kernel, index, grid, blocked, after, out_specs, out_shape, moved, flops, name, scratch=(), aliases=None):
    count = len(blocked)
    waits = len(after)
    outs = len(out_shape)

    def run(index_ref, *refs):
        kernel(index_ref, *refs[:count], *refs[count + waits : count + waits + outs], *refs[count + waits + outs + 1 :])
        refs[count + waits + outs][0, 0] = jnp.float32(0.0)

    result = pl.pallas_call(
        run,
        grid_spec=pltpu.PrefetchScalarGridSpec(
            num_scalar_prefetch=1,
            grid=grid,
            in_specs=[spec for _, spec in blocked] + [corner(x) for x in after],
            out_specs=list(out_specs) + [pl.BlockSpec((1, 1), lambda *_: (0, 0), memory_space=pltpu.SMEM)],
            scratch_shapes=list(scratch),
        ),
        out_shape=list(out_shape) + [jax.ShapeDtypeStruct((1, 1), jnp.float32)],
        input_output_aliases=aliases or {},
        compiler_params=params(),
        cost_estimate=cost(flops, moved),
        name=name,
    )(index, *[x for x, _ in blocked], *after)
    return result[:-1], result[-1].reshape(())


def tie(index, after):
    _, zero = call(lambda index_ref: None, index, (1,), [], after, [], [], 8192, 0, "tie")
    return zero


def forward(index, doc, q, k, v, kp, vp, weight):
    rows, feature = q.shape
    pairs = feature // HD // PAIR
    block = 512
    width = weight.shape[1] // 4
    blocks = width // block
    head = pl.BlockSpec((rows, PAIR * HD), lambda n, *_: (0, jnp.minimum(n, pairs - 1)))
    late = lambda n: jnp.maximum(n - pairs, 0)
    far = pl.BlockSpec((HALF, block), lambda n, *_: (0, late(n)))
    out = jax.ShapeDtypeStruct((HALF, width), jnp.bfloat16)
    return call(
        functools.partial(forward_kernel, pairs), index, (pairs + blocks,),
        [(doc, pl.BlockSpec(doc.shape, lambda n, *_: (0, 0)))] + [(x, head) for x in (q, k, v, kp, vp)]
        + [(weight, pl.BlockSpec((feature, block), lambda n, idx: (0, idx[0] * blocks + late(n))))], [],
        [head, pl.BlockSpec((PAIR, rows, rows), lambda n, *_: (jnp.minimum(n, pairs - 1), 0, 0)), far, far],
        [jax.ShapeDtypeStruct((rows, feature), jnp.bfloat16), jax.ShapeDtypeStruct((PAIR * pairs, rows, rows), jnp.bfloat16), out, out],
        2**23, 12 * 2 * 2**23 * PAIR * pairs, "attend",
        scratch=[pltpu.VMEM((rows, rows), jnp.float32), pltpu.VMEM((pairs, rows, PAIR * HD), jnp.bfloat16)],
    )


def project(weight, index, groups, total, after):
    rows = sum(piece[0].shape[0] for piece in groups[0])
    depth = groups[0][0][0].shape[1]
    out_rows = weight.shape[0]
    block = 256
    shape = [[(len(piece), piece[0].shape[0]) for piece in g] for g in groups]
    has_total = total is not None

    def kernel(index_ref, *refs):
        refs = list(refs)
        w = [refs.pop(0)[...] for _ in groups]
        out_ref = refs[-1]
        start = 0
        base = refs[-2] if has_total else None
        sums = {}
        for j, pieces in enumerate(shape):
            start = 0
            for many, height in pieces:
                x = refs.pop(0)[...]
                for _ in range(many - 1):
                    x = x + refs.pop(0)[...]
                term = nt(x, w[j])
                key = (start, height)
                at = pl.ds(start, height)
                if j == 0:
                    out_ref[at, :] = term + base[at, :] if has_total else term
                else:
                    out_ref[at, :] += term
                start += height

    blocked = [(weight, pl.BlockSpec((block, depth), lambda n, idx, j=j: (n, idx[j]))) for j in range(len(groups))]
    for g in groups:
        for piece in g:
            for x in piece:
                blocked.append((x, pl.BlockSpec(x.shape, lambda n, idx: (0, 0))))
    if has_total:
        blocked.append((total, pl.BlockSpec((rows, block), lambda n, idx: (0, n))))
    return call(
        kernel, index, (out_rows // block,), blocked, after,
        [pl.BlockSpec((rows, block), lambda n, idx: (0, n))],
        [jax.ShapeDtypeStruct((rows, out_rows), jnp.float32)],
        2 * out_rows * depth * len(groups), 2 * rows * depth * out_rows * len(groups), "project",
    )


def parts(weight, index, attended, count, after, stream=None):
    rows, depth = attended.shape
    width = weight.shape[1] // 4
    block = 512
    steps = width // block

    def kernel(index_ref, x_ref, *refs):
        base = count + (stream is not None)
        for j in range(count):
            out = nn(x_ref[...], refs[j][...])
            if stream is not None and j == count - 1:
                out = refs[count][...].astype(jnp.float32) - out
            out = out.astype(jnp.bfloat16)
            refs[base + 2 * j][...] = out[:HALF]
            refs[base + 2 * j + 1][...] = out[HALF:]

    blocked = [(attended, pl.BlockSpec((rows, depth), lambda n, idx: (0, 0)))]
    for j in range(count):
        blocked.append((weight, pl.BlockSpec((depth, block), lambda n, idx, j=j: (0, idx[j] * steps + n))))
    if stream is not None:
        blocked.append((stream, pl.BlockSpec((rows, block), lambda n, idx: (0, n))))
    return call(
        kernel, index, (steps,), blocked, after,
        [pl.BlockSpec((HALF, block), lambda n, idx: (0, n))] * (2 * count),
        [jax.ShapeDtypeStruct((HALF, width), jnp.bfloat16)] * (2 * count),
        count * 2 * depth * width, 2 * rows * depth * width * count, "parts",
    )


def place(index, whole, rows, piece, start, after):
    height, width = piece.shape
    blocked = [(piece, pl.BlockSpec((height, width), lambda n, idx: (0, 0)))]
    aliases = None
    if whole is not None:
        blocked.append((whole, ANY))
        aliases = {2: 0}

    def kernel(index_ref, x_ref, *refs):
        refs[-1][...] = x_ref[...]

    (out,), zero = call(
        kernel, index, (1,), blocked, after,
        [pl.BlockSpec((height, width), lambda n, idx: (start // height, 0))],
        [jax.ShapeDtypeStruct((rows, width), piece.dtype)],
        4 * height * width, 0, "place", aliases=aliases,
    )
    return out, zero


def settle(index, which, grads, k, v, back, after):
    height, width = k.shape
    wide = 512

    def kernel(index_ref, k_ref, v_ref, back_ref, *refs):
        gk_ref, gv_ref = refs[-2:]
        gk_ref[...] = (k_ref[...].astype(jnp.float32) + back_ref[0].astype(jnp.float32)).astype(jnp.bfloat16)
        gv_ref[...] = (v_ref[...].astype(jnp.float32) + back_ref[1].astype(jnp.float32)).astype(jnp.bfloat16)

    flat = pl.BlockSpec((height, wide), lambda n, idx: (0, n))
    out_spec = pl.BlockSpec((height, wide), lambda n, idx: (which, n))
    out = jax.ShapeDtypeStruct((2 * height, width), jnp.bfloat16)
    return call(
        kernel, index, (width // wide,),
        [(k, flat), (v, flat), (back, pl.BlockSpec((2, height, wide), lambda n, idx: (0, 0, n)))] + [(x, ANY) for x in grads],
        after, [out_spec, out_spec], [out, out],
        16 * height * width, 0, "settle", aliases={4: 0, 5: 1} if grads else None,
    )


def gate(index, x, after):
    (out,), _ = call(
        lambda *refs: None, index, (1,), [(x, ANY)], after, [ANY], [jax.ShapeDtypeStruct(x.shape, x.dtype)], 8192, 0, "gate", aliases={1: 0}
    )
    return out


def total_of(*terms):
    result = terms[0].astype(jnp.float32)
    for x in terms[1:]:
        result = result + x.astype(jnp.float32)
    return result


def backward(qb, weight, index, total, outer, middle, probs, attended, q, k, v, kp, vp, carried, after, steps, earlier=()):
    rows, feature = q.shape
    heads = feature // HD
    depth = outer.shape[1]
    wide = PAIR * HD
    scaling = HD ** (-0.5)
    bf = jnp.bfloat16
    first = steps[0]
    kept = list(earlier) if earlier else list(carried[:1])
    skip = len(after) + len(kept)

    def kernel(index_ref, w_ref, total_ref, outer_ref, middle_ref, p_ref, att_ref, q_ref, k_ref, v_ref, kp_ref, vp_ref, *refs):
        refs = refs[skip:]
        carry = refs[:4] if qb else ()
        dq_ref, send_ref, k0_ref, v0_ref, k1_ref, v1_ref, x_ref = refs[len(carry) :]

        @pl.when((pl.program_id(0) == 0) & (index_ref[1] == 1))
        def _():
            x_ref[...] = outer_ref[...]

        @pl.when((pl.program_id(0) == 0) & (index_ref[1] == 0))
        def _():
            x_ref[...] = middle_ref[...]

        qs = pl.ds(qb * HALF, HALF)
        ks = pl.ds((1 - qb) * HALF, HALF)
        tri = lower(HALF)
        d_out_pair = (total_ref[...] + nt(x_ref[...], w_ref[...])).astype(bf)
        for head in range(PAIR):
            cols = pl.ds(head * HD, HD)
            d_out = d_out_pair[:, head * HD : (head + 1) * HD]
            row_delta = jnp.sum(
                d_out.astype(jnp.float32) * att_ref[:, cols].astype(jnp.float32), axis=1, keepdims=True
            )
            qh = q_ref[:, cols]
            k_rest_ref, v_rest_ref = (k_ref, v_ref) if qb else (kp_ref, vp_ref)
            k_rest, v_rest = k_rest_ref[ks, cols], v_rest_ref[ks, cols]
            own, prev = (qs, pl.ds(0, HALF)) if qb else (pl.ds(0, HALF), qs)
            p_diag = p_ref[head, :, qb * HALF : (qb + 1) * HALF].astype(jnp.float32)
            p_rest = p_ref[head, :, (1 - qb) * HALF : (2 - qb) * HALF]
            dp_diag = jnp.where(tri, nt(d_out, v_ref[own, cols]), nt(d_out, vp_ref[prev, cols]))
            dp_rest = nt(d_out, v_rest)
            ds_diag = p_diag * (dp_diag - row_delta)
            ds_rest = (p_rest.astype(jnp.float32) * (dp_rest - row_delta)).astype(bf)
            ds_own = jnp.where(tri, ds_diag, 0.0).astype(bf)
            ds_before = jnp.where(tri, 0.0, ds_diag).astype(bf)
            p_own = jnp.where(tri, p_diag, 0.0).astype(bf)
            p_before = jnp.where(tri, 0.0, p_diag).astype(bf)
            dq = nn(ds_own, k_ref[own, cols]) + nn(ds_before, kp_ref[prev, cols]) + nn(ds_rest, k_rest)
            dq_ref[:, cols] = (dq * scaling).astype(bf)
            dk_own, dv_own = tn(ds_own, qh) * scaling, tn(p_own, d_out)
            dk_before, dv_before = tn(ds_before, qh) * scaling, tn(p_before, d_out)
            dk_rest, dv_rest = tn(ds_rest, qh) * scaling, tn(p_rest, d_out)
            if qb == 0:
                send_ref[0, :, cols] = dk_before.astype(bf)
                send_ref[1, :, cols] = dv_before.astype(bf)
                k0_ref[:, cols], v0_ref[:, cols] = dk_own.astype(bf), dv_own.astype(bf)
                k1_ref[:, cols], v1_ref[:, cols] = dk_rest.astype(bf), dv_rest.astype(bf)
            else:
                k0i, v0i, kri, vri = carry
                send_ref[0, :, cols] = (dk_before + kri[:, cols].astype(jnp.float32)).astype(bf)
                send_ref[1, :, cols] = (dv_before + vri[:, cols].astype(jnp.float32)).astype(bf)
                k0_ref[:, cols] = (dk_rest + k0i[:, cols].astype(jnp.float32)).astype(bf)
                v0_ref[:, cols] = (dv_rest + v0i[:, cols].astype(jnp.float32)).astype(bf)
                k1_ref[:, cols], v1_ref[:, cols] = dk_own.astype(bf), dv_own.astype(bf)

    whole = pl.BlockSpec((rows, wide), lambda h, *_: (0, first + h))
    half = pl.BlockSpec((HALF, wide), lambda h, *_: (0, first + h))
    mine = pl.BlockSpec((HALF, wide), lambda h, *_: (qb, first + h))
    blocked = [
        (weight, pl.BlockSpec((wide, depth), lambda h, idx: (first + h, idx[0]))),
        (total, mine),
        (outer, pl.BlockSpec((HALF, depth), lambda h, *_: (0, 0))),
        (middle, pl.BlockSpec((HALF, depth), lambda h, *_: (qb, 0))),
        (probs, pl.BlockSpec((PAIR, HALF, rows), lambda h, *_: (first + h, qb, 0))),
        (attended, mine),
        (q, mine),
        (k, whole if qb else mine),
        (v, whole if qb else mine),
        (kp, mine if qb else whole),
        (vp, mine if qb else whole),
    ]
    aliases = {1 + len(blocked) + i: i for i in range(len(kept))}
    pair = pl.BlockSpec((2, HALF, wide), lambda h, *_: (0, 0, first + h))
    blocked += [(x, ANY) for x in kept] + [(x, corner(x)) for x in after] + [(x, half) for x in carried[1:]]
    half_out = jax.ShapeDtypeStruct((HALF, feature), bf)
    whole_out = jax.ShapeDtypeStruct((rows, feature), bf)
    return call(
        kernel, index, (steps[1] - first,), blocked, [],
        [mine, pair] + [half] * 4,
        [whole_out, jax.ShapeDtypeStruct((2, HALF, feature), bf)] + [half_out] * 4,
        16 * 2**20, 2 * HALF * depth * feature * 3, "backward", aliases=aliases,
        scratch=[pltpu.VMEM((HALF, depth), bf)],
    )


def from_behind(block, axis, distance):
    devices = range(lax.axis_size(axis))
    route = [(i - distance, i) for i in devices if i - distance in devices]
    return lax.ppermute(block, axis, route)


def shifted(block, axis, distance):
    count = lax.axis_size(axis)
    return lax.ppermute(block, axis, [((i - distance) % count, i) for i in range(count)])


def hop(block, pairs, name):
    with jax.named_scope(name):
        return lax.ppermute(block, "tp", pairs)


def body(queries, keys, values, stream, grad_stream, out_proj, doc_ids):
    q, k, v, weight = queries[0], keys[0], values[0], out_proj[0]
    grad = grad_stream[0]
    rows, feature = q.shape
    chunks = rows // HALF
    me = lax.axis_index("tp").astype(jnp.int32)
    ctx = lax.axis_index("ctx").astype(jnp.int32)
    near, across, far = me ^ 1, me ^ 2, 3 - me
    one = lambda x: x.reshape(1)

    idx = one(me)
    end = (me == 0) | (me == 3)
    bf = jnp.bfloat16
    half = lambda x, c: x[c * HALF : (c + 1) * HALF]
    both = range(chunks)

    kp = from_behind(k, "ctx", 1)
    vp = from_behind(v, "ctx", 1)
    o1 = hop(grad, OUTER, "outer1")
    m1 = hop(grad, MIDDLE, "middle1")
    grad_next = shifted(grad, "pipe", -1)
    (attended, probs, *pa), zero = forward(jnp.stack([far, ctx]), doc_ids, q, k, v, kp, vp, weight)
    o1 = gate(idx, o1, [attended])
    m2 = hop(o1, MIDDLE, "middle2")
    to_x2 = []
    for c in both:
        to_x2.append(total_of(jnp.where(end, pa[c], half(m1, c)), zero).astype(bf))
        zero = tie(idx, [to_x2[c]])
    x2 = [hop(x, OUTER, f"outer2{'ab'[c]}") for c, x in enumerate(to_x2)]
    (pb0, pb1, pc0, pc1, pd0, pd1), _ = parts(weight, jnp.stack([across, near, me]), attended, 3, to_x2, stream[0])
    pb, pc, pd = (pb0, pb1), (pc0, pc1), (pd0, pd1)
    (total,), zero = project(weight, jnp.stack([me, near]), [[(grad,)], [(o1,)]], None, [pb0])
    n3, x3 = [], []
    for c in both:
        to_n3 = total_of(pb[c], x2[c], zero).astype(bf)
        to_x3 = total_of(jnp.where(end, pb[c], half(m2, c)), zero).astype(bf)
        n3.append(hop(to_n3, MIDDLE, f"middle3{'ab'[c]}"))
        x3.append(hop(to_x3, OUTER, f"outer3{'ab'[c]}"))
        if c == 0:
            zero = tie(idx, [to_n3, to_x3])
    (total,), zero = project(
        weight, one(across), [[(jnp.where(end, x2[c], half(m2, c)),) for c in both]], total, [to_n3, to_x3]
    )
    next_grad, zero = place(idx, None, 2 * HALF, grad_next, 0, [total])
    far_and_end = jnp.stack([far, end.astype(jnp.int32)])
    hops = {}

    def launch(p, zero):
        at, height = PIECES[p]
        c = at // HALF
        piece = slice(at - c * HALF, at - c * HALF + height)
        to_f4 = total_of(pc[c][piece], n3[c][piece], zero).astype(bf)
        to_n4 = total_of(pa[c][piece], x3[c][piece], zero).astype(bf)
        hops[p] = (hop(to_f4, OUTER, f"outer4{'abcd'[p]}"), hop(to_n4, MIDDLE, f"middle4{'abcd'[p]}"))
        return [to_f4, to_n4]

    arrived, done = [], []

    def finish(p, zero):
        at, height = PIECES[p]
        c = at // HALF
        own = pd[c][at - c * HALF : at - c * HALF + height]
        rebuilt = (own.astype(jnp.float32) - total_of(*hops[p], zero)).astype(bf)
        arrived.append(shifted(rebuilt, "pipe", -1))
        done.append(rebuilt)
        return tie(idx, [rebuilt])

    pairs = feature // HD // PAIR
    run = lambda c, *rest: backward(c, weight, far_and_end, total, x3[c], m1, probs, attended, q, k, v, kp, vp, *rest)
    sends = launch(0, zero)
    (dq, send0, k0, v0, k1, v1), zero = run(0, (), sends, (0, pairs))
    back0 = from_behind(send0, "ctx", -1)
    zero = tie(idx, [n3[1], x3[1], dq])
    sends = launch(1, zero)
    (dq, send1, k0, v0, k1, v1), zero = run(1, (dq, k0, v0, k1, v1), sends, (0, pairs))
    zero = finish(0, zero)
    grads, zero = settle(idx, 0, [], k0, v0, back0, [done[0]])
    zero = tie(idx, launch(2, zero))
    zero = finish(1, zero)
    back1 = from_behind(gate(idx, send1, [done[1]]), "ctx", -1)
    finish(2, zero)
    stream_next, zero = place(idx, None, 2 * HALF, arrived[0], 0, [done[2]])
    (grad_keys, grad_values), _ = settle(idx, 1, grads, k1, v1, back1, [stream_next])
    after = [grad_keys]
    for (at, height), piece in list(zip(PIECES, arrived))[1:]:
        stream_next, _ = place(idx, stream_next, 2 * HALF, piece, at, after)
        after = []
    return tuple(x[None] for x in (dq, grad_keys, grad_values, stream_next, next_grad))


def solution(mesh):
    cut = P("pipe", "ctx", "tp")
    in_specs = (cut, cut, cut, cut, cut, P("pipe", "tp", None), P("pipe", None))
    out_specs = (cut, cut, cut, cut, cut)
    return jax.shard_map(body, mesh=mesh, in_specs=in_specs, out_specs=out_specs, check_vma=False)
```

```python
import functools

import jax
import jax.numpy as jnp
from jax import lax
from jax.experimental import pallas as pl
from jax.experimental.pallas import tpu as pltpu
from jax.sharding import PartitionSpec as P

HD = 128
WINDOW = 512
NEG = -1e30
HALF = 256
PIECES = [(0, 256), (256, 128), (384, 128)]
PAIR = 4
VMEM_LIMIT = 44 * 1024 * 1024
COST = 1.0

OUTER = [(0, 1), (1, 0), (2, 3), (3, 2)]
MIDDLE = [(1, 2), (2, 1)]
OUTER_INWARD = [(0, 1), (3, 2)]
OUTER_OUTWARD = [(1, 0), (2, 3)]


def params():
    return pltpu.CompilerParams(vmem_limit_bytes=VMEM_LIMIT)


def dot(a, b, contract):
    return lax.dot_general(a, b, ((contract[0], contract[1]), ((), ())), preferred_element_type=jnp.float32)


def nt(a, b):
    return dot(a, b, ((1,), (1,)))


def nn(a, b):
    return dot(a, b, ((1,), (0,)))


def tn(a, b):
    return dot(a, b, ((0,), (0,)))


def lower(size):
    row = lax.broadcasted_iota(jnp.int32, (size, size), 0)
    col = lax.broadcasted_iota(jnp.int32, (size, size), 1)
    return col <= row


def forward_kernel(steps, index_ref, doc_ref, q_ref, k_ref, v_ref, kp_ref, vp_ref, far_ref, att_ref, w_ref, far0_ref, far1_ref, bias_ref, all_ref):
    rows = q_ref.shape[0]
    step = pl.program_id(0)
    scaling = HD ** (-0.5)

    @pl.when(step == 0)
    def _():
        index = index_ref[1]
        own = doc_ref[:, pl.ds(pl.multiple_of(index * rows, rows), rows)]
        before = doc_ref[:, pl.ds(pl.multiple_of(jnp.maximum(index - 1, 0) * rows, rows), rows)]
        before = jnp.where(index > 0, before, -1)
        own = jnp.broadcast_to(own, (rows, rows))
        before = jnp.broadcast_to(before, (rows, rows))
        key_doc = jnp.where(lower(rows), own, before)
        bias_ref[...] = jnp.where(key_doc == own.T, 0.0, NEG)

    @pl.when(step < steps)
    def _():
        tri = lower(HALF)
        for head in range(q_ref.shape[1] // HD):
            cols = pl.ds(head * HD, HD)
            for qb in range(2):
                qs = pl.ds(qb * HALF, HALF)
                ks = pl.ds((1 - qb) * HALF, HALF)
                q = q_ref[qs, cols]
                diagonal = jnp.where(tri, nt(q, k_ref[qs, cols]), nt(q, kp_ref[qs, cols]))
                if qb == 0:
                    scores = jnp.concatenate([diagonal, nt(q, kp_ref[ks, cols])], 1)
                else:
                    scores = jnp.concatenate([nt(q, k_ref[ks, cols]), diagonal], 1)
                scores = scores * scaling + bias_ref[qs, :]
                row_max = jnp.max(scores, axis=1, keepdims=True)
                exponent = jnp.exp(scores - row_max)
                row_sum = jnp.sum(exponent, axis=1, keepdims=True)
                prob = exponent * (1.0 / row_sum)
                w_ref[head, qs, :] = prob.astype(jnp.bfloat16)
                mine = prob[:, qb * HALF : (qb + 1) * HALF]
                rest = prob[:, (1 - qb) * HALF : (2 - qb) * HALF].astype(jnp.bfloat16)
                mine_own = jnp.where(tri, mine, 0.0).astype(jnp.bfloat16)
                mine_before = jnp.where(tri, 0.0, mine).astype(jnp.bfloat16)
                att = nn(mine_own, v_ref[qs, cols]) + nn(mine_before, vp_ref[qs, cols])
                att = att + nn(rest, (vp_ref if qb == 0 else v_ref)[ks, cols])
                att_ref[qs, cols] = att.astype(jnp.bfloat16)

    for j in range(steps):

        @pl.when(step == j)
        def _():
            all_ref[j] = att_ref[...]

    @pl.when(step >= steps)
    def _():
        wide = PAIR * HD
        out = nn(all_ref[0], far_ref[:wide, :])
        for j in range(1, steps):
            out += nn(all_ref[j], far_ref[j * wide : (j + 1) * wide, :])
        out = out.astype(jnp.bfloat16)
        far0_ref[...] = out[:HALF]
        far1_ref[...] = out[HALF:]


def cost(flops, moved, transcendentals=0):
    return pl.CostEstimate(flops=int(flops * COST), bytes_accessed=int(moved * COST), transcendentals=int(transcendentals * COST))


ANY = pl.BlockSpec(memory_space=pl.ANY)


def corner(x):
    block = (1,) * (x.ndim - 2) + (16, HD)
    return pl.BlockSpec(block, lambda *_: (0,) * x.ndim)


def call(kernel, index, grid, blocked, after, out_specs, out_shape, moved, flops, name, scratch=(), aliases=None):
    count = len(blocked)
    waits = len(after)
    outs = len(out_shape)

    def run(index_ref, *refs):
        kernel(index_ref, *refs[:count], *refs[count + waits : count + waits + outs], *refs[count + waits + outs + 1 :])
        refs[count + waits + outs][0, 0] = jnp.float32(0.0)

    result = pl.pallas_call(
        run,
        grid_spec=pltpu.PrefetchScalarGridSpec(
            num_scalar_prefetch=1,
            grid=grid,
            in_specs=[spec for _, spec in blocked] + [corner(x) for x in after],
            out_specs=list(out_specs) + [pl.BlockSpec((1, 1), lambda *_: (0, 0), memory_space=pltpu.SMEM)],
            scratch_shapes=list(scratch),
        ),
        out_shape=list(out_shape) + [jax.ShapeDtypeStruct((1, 1), jnp.float32)],
        input_output_aliases=aliases or {},
        compiler_params=params(),
        cost_estimate=cost(flops, moved),
        name=name,
    )(index, *[x for x, _ in blocked], *after)
    return result[:-1], result[-1].reshape(())


def tie(index, after):
    _, zero = call(lambda index_ref: None, index, (1,), [], after, [], [], 8192, 0, "tie")
    return zero


def forward(index, doc, q, k, v, kp, vp, weight):
    rows, feature = q.shape
    pairs = feature // HD // PAIR
    block = 512
    width = weight.shape[1] // 4
    blocks = width // block
    head = pl.BlockSpec((rows, PAIR * HD), lambda n, *_: (0, jnp.minimum(n, pairs - 1)))
    late = lambda n: jnp.maximum(n - pairs, 0)
    far = pl.BlockSpec((HALF, block), lambda n, *_: (0, late(n)))
    out = jax.ShapeDtypeStruct((HALF, width), jnp.bfloat16)
    return call(
        functools.partial(forward_kernel, pairs), index, (pairs + blocks,),
        [(doc, pl.BlockSpec(doc.shape, lambda n, *_: (0, 0)))] + [(x, head) for x in (q, k, v, kp, vp)]
        + [(weight, pl.BlockSpec((feature, block), lambda n, idx: (0, idx[0] * blocks + late(n))))], [],
        [head, pl.BlockSpec((PAIR, rows, rows), lambda n, *_: (jnp.minimum(n, pairs - 1), 0, 0)), far, far],
        [jax.ShapeDtypeStruct((rows, feature), jnp.bfloat16), jax.ShapeDtypeStruct((PAIR * pairs, rows, rows), jnp.bfloat16), out, out],
        2**23, 12 * 2 * 2**23 * PAIR * pairs, "attend",
        scratch=[pltpu.VMEM((rows, rows), jnp.float32), pltpu.VMEM((pairs, rows, PAIR * HD), jnp.bfloat16)],
    )


def project(weight, index, groups, total, after):
    rows = sum(piece[0].shape[0] for piece in groups[0])
    depth = groups[0][0][0].shape[1]
    out_rows = weight.shape[0]
    block = 256
    shape = [[(len(piece), piece[0].shape[0]) for piece in g] for g in groups]
    has_total = total is not None

    def kernel(index_ref, *refs):
        refs = list(refs)
        w = [refs.pop(0)[...] for _ in groups]
        out_ref = refs[-1]
        start = 0
        base = refs[-2] if has_total else None
        sums = {}
        for j, pieces in enumerate(shape):
            start = 0
            for many, height in pieces:
                x = refs.pop(0)[...]
                for _ in range(many - 1):
                    x = x + refs.pop(0)[...]
                term = nt(x, w[j])
                key = (start, height)
                at = pl.ds(start, height)
                if j == 0:
                    out_ref[at, :] = term + base[at, :] if has_total else term
                else:
                    out_ref[at, :] += term
                start += height

    blocked = [(weight, pl.BlockSpec((block, depth), lambda n, idx, j=j: (n, idx[j]))) for j in range(len(groups))]
    for g in groups:
        for piece in g:
            for x in piece:
                blocked.append((x, pl.BlockSpec(x.shape, lambda n, idx: (0, 0))))
    if has_total:
        blocked.append((total, pl.BlockSpec((rows, block), lambda n, idx: (0, n))))
    return call(
        kernel, index, (out_rows // block,), blocked, after,
        [pl.BlockSpec((rows, block), lambda n, idx: (0, n))],
        [jax.ShapeDtypeStruct((rows, out_rows), jnp.float32)],
        2 * out_rows * depth * len(groups), 2 * rows * depth * out_rows * len(groups), "project",
    )


def parts(weight, index, attended, count, after, stream=None):
    rows, depth = attended.shape
    width = weight.shape[1] // 4
    block = 512
    steps = width // block

    def kernel(index_ref, x_ref, *refs):
        base = count + (stream is not None)
        for j in range(count):
            out = nn(x_ref[...], refs[j][...])
            if stream is not None and j == count - 1:
                out = refs[count][...].astype(jnp.float32) - out
            out = out.astype(jnp.bfloat16)
            refs[base + 2 * j][...] = out[:HALF]
            refs[base + 2 * j + 1][...] = out[HALF:]

    blocked = [(attended, pl.BlockSpec((rows, depth), lambda n, idx: (0, 0)))]
    for j in range(count):
        blocked.append((weight, pl.BlockSpec((depth, block), lambda n, idx, j=j: (0, idx[j] * steps + n))))
    if stream is not None:
        blocked.append((stream, pl.BlockSpec((rows, block), lambda n, idx: (0, n))))
    return call(
        kernel, index, (steps,), blocked, after,
        [pl.BlockSpec((HALF, block), lambda n, idx: (0, n))] * (2 * count),
        [jax.ShapeDtypeStruct((HALF, width), jnp.bfloat16)] * (2 * count),
        count * 2 * depth * width, 2 * rows * depth * width * count, "parts",
    )


def place(index, whole, rows, piece, start, after):
    height, width = piece.shape
    blocked = [(piece, pl.BlockSpec((height, width), lambda n, idx: (0, 0)))]
    aliases = None
    if whole is not None:
        blocked.append((whole, ANY))
        aliases = {2: 0}

    def kernel(index_ref, x_ref, *refs):
        refs[-1][...] = x_ref[...]

    (out,), zero = call(
        kernel, index, (1,), blocked, after,
        [pl.BlockSpec((height, width), lambda n, idx: (start // height, 0))],
        [jax.ShapeDtypeStruct((rows, width), piece.dtype)],
        4 * height * width, 0, "place", aliases=aliases,
    )
    return out, zero


def settle(index, which, grads, k, v, back, after):
    height, width = k.shape
    wide = 512

    def kernel(index_ref, k_ref, v_ref, back_ref, *refs):
        gk_ref, gv_ref = refs[-2:]
        gk_ref[...] = (k_ref[...].astype(jnp.float32) + back_ref[0].astype(jnp.float32)).astype(jnp.bfloat16)
        gv_ref[...] = (v_ref[...].astype(jnp.float32) + back_ref[1].astype(jnp.float32)).astype(jnp.bfloat16)

    flat = pl.BlockSpec((height, wide), lambda n, idx: (0, n))
    out_spec = pl.BlockSpec((height, wide), lambda n, idx: (which, n))
    out = jax.ShapeDtypeStruct((2 * height, width), jnp.bfloat16)
    return call(
        kernel, index, (width // wide,),
        [(k, flat), (v, flat), (back, pl.BlockSpec((2, height, wide), lambda n, idx: (0, 0, n)))] + [(x, ANY) for x in grads],
        after, [out_spec, out_spec], [out, out],
        16 * height * width, 0, "settle", aliases={4: 0, 5: 1} if grads else None,
    )


def gate(index, x, after):
    (out,), _ = call(
        lambda *refs: None, index, (1,), [(x, ANY)], after, [ANY], [jax.ShapeDtypeStruct(x.shape, x.dtype)], 8192, 0, "gate", aliases={1: 0}
    )
    return out


def total_of(*terms):
    result = terms[0].astype(jnp.float32)
    for x in terms[1:]:
        result = result + x.astype(jnp.float32)
    return result


def backward(qb, weight, index, total, outer, middle, probs, attended, q, k, v, kp, vp, carried, after, steps, earlier=()):
    rows, feature = q.shape
    heads = feature // HD
    depth = outer.shape[1]
    wide = PAIR * HD
    scaling = HD ** (-0.5)
    bf = jnp.bfloat16
    first = steps[0]
    kept = list(earlier) if earlier else list(carried[:1])
    skip = len(after) + len(kept)

    def kernel(index_ref, w_ref, total_ref, outer_ref, middle_ref, p_ref, att_ref, q_ref, k_ref, v_ref, kp_ref, vp_ref, *refs):
        refs = refs[skip:]
        carry = refs[:4] if qb else ()
        dq_ref, send_ref, k0_ref, v0_ref, k1_ref, v1_ref, x_ref = refs[len(carry) :]

        @pl.when((pl.program_id(0) == 0) & (index_ref[1] == 1))
        def _():
            x_ref[...] = outer_ref[...]

        @pl.when((pl.program_id(0) == 0) & (index_ref[1] == 0))
        def _():
            x_ref[...] = middle_ref[...]

        qs = pl.ds(qb * HALF, HALF)
        ks = pl.ds((1 - qb) * HALF, HALF)
        tri = lower(HALF)
        d_out_pair = (total_ref[...] + nt(x_ref[...], w_ref[...])).astype(bf)
        for head in range(PAIR):
            cols = pl.ds(head * HD, HD)
            d_out = d_out_pair[:, head * HD : (head + 1) * HD]
            row_delta = jnp.sum(
                d_out.astype(jnp.float32) * att_ref[:, cols].astype(jnp.float32), axis=1, keepdims=True
            )
            qh = q_ref[:, cols]
            k_rest_ref, v_rest_ref = (k_ref, v_ref) if qb else (kp_ref, vp_ref)
            k_rest, v_rest = k_rest_ref[ks, cols], v_rest_ref[ks, cols]
            own, prev = (qs, pl.ds(0, HALF)) if qb else (pl.ds(0, HALF), qs)
            p_diag = p_ref[head, :, qb * HALF : (qb + 1) * HALF].astype(jnp.float32)
            p_rest = p_ref[head, :, (1 - qb) * HALF : (2 - qb) * HALF]
            dp_diag = jnp.where(tri, nt(d_out, v_ref[own, cols]), nt(d_out, vp_ref[prev, cols]))
            dp_rest = nt(d_out, v_rest)
            ds_diag = p_diag * (dp_diag - row_delta)
            ds_rest = (p_rest.astype(jnp.float32) * (dp_rest - row_delta)).astype(bf)
            ds_own = jnp.where(tri, ds_diag, 0.0).astype(bf)
            ds_before = jnp.where(tri, 0.0, ds_diag).astype(bf)
            p_own = jnp.where(tri, p_diag, 0.0).astype(bf)
            p_before = jnp.where(tri, 0.0, p_diag).astype(bf)
            dq = nn(ds_own, k_ref[own, cols]) + nn(ds_before, kp_ref[prev, cols]) + nn(ds_rest, k_rest)
            dq_ref[:, cols] = (dq * scaling).astype(bf)
            dk_own, dv_own = tn(ds_own, qh) * scaling, tn(p_own, d_out)
            dk_before, dv_before = tn(ds_before, qh) * scaling, tn(p_before, d_out)
            dk_rest, dv_rest = tn(ds_rest, qh) * scaling, tn(p_rest, d_out)
            if qb == 0:
                send_ref[0, :, cols] = dk_before.astype(bf)
                send_ref[1, :, cols] = dv_before.astype(bf)
                k0_ref[:, cols], v0_ref[:, cols] = dk_own.astype(bf), dv_own.astype(bf)
                k1_ref[:, cols], v1_ref[:, cols] = dk_rest.astype(bf), dv_rest.astype(bf)
            else:
                k0i, v0i, kri, vri = carry
                send_ref[0, :, cols] = (dk_before + kri[:, cols].astype(jnp.float32)).astype(bf)
                send_ref[1, :, cols] = (dv_before + vri[:, cols].astype(jnp.float32)).astype(bf)
                k0_ref[:, cols] = (dk_rest + k0i[:, cols].astype(jnp.float32)).astype(bf)
                v0_ref[:, cols] = (dv_rest + v0i[:, cols].astype(jnp.float32)).astype(bf)
                k1_ref[:, cols], v1_ref[:, cols] = dk_own.astype(bf), dv_own.astype(bf)

    whole = pl.BlockSpec((rows, wide), lambda h, *_: (0, first + h))
    half = pl.BlockSpec((HALF, wide), lambda h, *_: (0, first + h))
    mine = pl.BlockSpec((HALF, wide), lambda h, *_: (qb, first + h))
    blocked = [
        (weight, pl.BlockSpec((wide, depth), lambda h, idx: (first + h, idx[0]))),
        (total, mine),
        (outer, pl.BlockSpec((HALF, depth), lambda h, *_: (0, 0))),
        (middle, pl.BlockSpec((HALF, depth), lambda h, *_: (qb, 0))),
        (probs, pl.BlockSpec((PAIR, HALF, rows), lambda h, *_: (first + h, qb, 0))),
        (attended, mine),
        (q, mine),
        (k, whole if qb else mine),
        (v, whole if qb else mine),
        (kp, mine if qb else whole),
        (vp, mine if qb else whole),
    ]
    aliases = {1 + len(blocked) + i: i for i in range(len(kept))}
    pair = pl.BlockSpec((2, HALF, wide), lambda h, *_: (0, 0, first + h))
    blocked += [(x, ANY) for x in kept] + [(x, corner(x)) for x in after] + [(x, half) for x in carried[1:]]
    half_out = jax.ShapeDtypeStruct((HALF, feature), bf)
    whole_out = jax.ShapeDtypeStruct((rows, feature), bf)
    return call(
        kernel, index, (steps[1] - first,), blocked, [],
        [mine, pair] + [half] * 4,
        [whole_out, jax.ShapeDtypeStruct((2, HALF, feature), bf)] + [half_out] * 4,
        16 * 2**20, 2 * HALF * depth * feature * 3, "backward", aliases=aliases,
        scratch=[pltpu.VMEM((HALF, depth), bf)],
    )


def from_behind(block, axis, distance):
    devices = range(lax.axis_size(axis))
    route = [(i - distance, i) for i in devices if i - distance in devices]
    return lax.ppermute(block, axis, route)


def shifted(block, axis, distance):
    count = lax.axis_size(axis)
    return lax.ppermute(block, axis, [((i - distance) % count, i) for i in range(count)])


def hop(block, pairs, name):
    with jax.named_scope(name):
        return lax.ppermute(block, "tp", pairs)


def body(queries, keys, values, stream, grad_stream, out_proj, doc_ids):
    q, k, v, weight = queries[0], keys[0], values[0], out_proj[0]
    grad = grad_stream[0]
    rows, feature = q.shape
    chunks = rows // HALF
    me = lax.axis_index("tp").astype(jnp.int32)
    ctx = lax.axis_index("ctx").astype(jnp.int32)
    near, across, far = me ^ 1, me ^ 2, 3 - me
    one = lambda x: x.reshape(1)

    idx = one(me)
    end = (me == 0) | (me == 3)
    bf = jnp.bfloat16
    half = lambda x, c: x[c * HALF : (c + 1) * HALF]
    both = range(chunks)

    kp = from_behind(k, "ctx", 1)
    vp = from_behind(v, "ctx", 1)
    o1 = hop(grad, OUTER, "outer1")
    m1 = hop(grad, MIDDLE, "middle1")
    grad_next = shifted(grad, "pipe", -1)
    (attended, probs, *pa), zero = forward(jnp.stack([far, ctx]), doc_ids, q, k, v, kp, vp, weight)
    o1 = gate(idx, o1, [attended])
    m2 = hop(o1, MIDDLE, "middle2")
    to_x2 = []
    for c in both:
        to_x2.append(total_of(jnp.where(end, pa[c], half(m1, c)), zero).astype(bf))
        zero = tie(idx, [to_x2[c]])
    x2 = [hop(x, OUTER, f"outer2{'ab'[c]}") for c, x in enumerate(to_x2)]
    (pb0, pb1, pc0, pc1, pd0, pd1), _ = parts(weight, jnp.stack([across, near, me]), attended, 3, to_x2, stream[0])
    pb, pc, pd = (pb0, pb1), (pc0, pc1), (pd0, pd1)
    (total,), zero = project(weight, jnp.stack([me, near]), [[(grad,)], [(o1,)]], None, [pb0])
    n3, x3 = [], []
    for c in both:
        to_n3 = total_of(pb[c], x2[c], zero).astype(bf)
        to_x3 = total_of(jnp.where(end, pb[c], half(m2, c)), zero).astype(bf)
        n3.append(hop(to_n3, MIDDLE, f"middle3{'ab'[c]}"))
        x3.append(hop(to_x3, OUTER, f"outer3{'ab'[c]}"))
        if c == 0:
            zero = tie(idx, [to_n3, to_x3])
    (total,), zero = project(
        weight, one(across), [[(jnp.where(end, x2[c], half(m2, c)),) for c in both]], total, [to_n3, to_x3]
    )
    next_grad, zero = place(idx, None, 2 * HALF, grad_next, 0, [total])
    far_and_end = jnp.stack([far, end.astype(jnp.int32)])
    hops = {}

    def launch(p, zero):
        at, height = PIECES[p]
        c = at // HALF
        piece = slice(at - c * HALF, at - c * HALF + height)
        to_f4 = total_of(pc[c][piece], n3[c][piece], zero).astype(bf)
        to_n4 = total_of(pa[c][piece], x3[c][piece], zero).astype(bf)
        hops[p] = (hop(to_f4, OUTER, f"outer4{'abcd'[p]}"), hop(to_n4, MIDDLE, f"middle4{'abcd'[p]}"))
        return [to_f4, to_n4]

    arrived, done = [], []

    def finish(p, zero):
        at, height = PIECES[p]
        c = at // HALF
        own = pd[c][at - c * HALF : at - c * HALF + height]
        rebuilt = (own.astype(jnp.float32) - total_of(*hops[p], zero)).astype(bf)
        arrived.append(shifted(rebuilt, "pipe", -1))
        done.append(rebuilt)
        return tie(idx, [rebuilt])

    pairs = feature // HD // PAIR
    run = lambda c, *rest: backward(c, weight, far_and_end, total, x3[c], m1, probs, attended, q, k, v, kp, vp, *rest)
    sends = launch(0, zero)
    (dq, send0, k0, v0, k1, v1), zero = run(0, (), sends, (0, pairs))
    back0 = from_behind(send0, "ctx", -1)
    zero = tie(idx, [n3[1], x3[1], dq])
    sends = launch(1, zero)
    (dq, send1, k0, v0, k1, v1), zero = run(1, (dq, k0, v0, k1, v1), sends, (0, pairs))
    zero = finish(0, zero)
    grads, zero = settle(idx, 0, [], k0, v0, back0, [done[0]])
    zero = tie(idx, launch(2, zero))
    zero = finish(1, zero)
    back1 = from_behind(gate(idx, send1, [done[1]]), "ctx", -1)
    finish(2, zero)
    stream_next, zero = place(idx, None, 2 * HALF, arrived[0], 0, [done[2]])
    (grad_keys, grad_values), _ = settle(idx, 1, grads, k1, v1, back1, [stream_next])
    after = [grad_keys]
    for (at, height), piece in list(zip(PIECES, arrived))[1:]:
        stream_next, _ = place(idx, stream_next, 2 * HALF, piece, at, after)
        after = []
    return tuple(x[None] for x in (dq, grad_keys, grad_values, stream_next, next_grad))


def solution(mesh):
    cut = P("pipe", "ctx", "tp")
    in_specs = (cut, cut, cut, cut, cut, P("pipe", "tp", None), P("pipe", None))
    out_specs = (cut, cut, cut, cut, cut)
    return jax.shard_map(body, mesh=mesh, in_specs=in_specs, out_specs=out_specs, check_vma=False)
```

```python
import functools

import jax
import jax.numpy as jnp
from jax import lax
from jax.experimental import pallas as pl
from jax.experimental.pallas import tpu as pltpu
from jax.sharding import PartitionSpec as P

HD = 128
WINDOW = 512
NEG = -1e30
HALF = 256
PIECES = [(0, 256), (256, 128), (384, 128)]
PAIR = 4
VMEM_LIMIT = 42 * 1024 * 1024
COST = 1.0

OUTER = [(0, 1), (1, 0), (2, 3), (3, 2)]
MIDDLE = [(1, 2), (2, 1)]
OUTER_INWARD = [(0, 1), (3, 2)]
OUTER_OUTWARD = [(1, 0), (2, 3)]


def params():
    return pltpu.CompilerParams(vmem_limit_bytes=VMEM_LIMIT)


def dot(a, b, contract):
    return lax.dot_general(a, b, ((contract[0], contract[1]), ((), ())), preferred_element_type=jnp.float32)


def nt(a, b):
    return dot(a, b, ((1,), (1,)))


def nn(a, b):
    return dot(a, b, ((1,), (0,)))


def tn(a, b):
    return dot(a, b, ((0,), (0,)))


def lower(size):
    row = lax.broadcasted_iota(jnp.int32, (size, size), 0)
    col = lax.broadcasted_iota(jnp.int32, (size, size), 1)
    return col <= row


def forward_kernel(steps, index_ref, doc_ref, q_ref, k_ref, v_ref, kp_ref, vp_ref, far_ref, att_ref, w_ref, far0_ref, far1_ref, bias_ref, all_ref):
    rows = q_ref.shape[0]
    step = pl.program_id(0)
    scaling = HD ** (-0.5)

    @pl.when(step == 0)
    def _():
        index = index_ref[1]
        own = doc_ref[:, pl.ds(pl.multiple_of(index * rows, rows), rows)]
        before = doc_ref[:, pl.ds(pl.multiple_of(jnp.maximum(index - 1, 0) * rows, rows), rows)]
        before = jnp.where(index > 0, before, -1)
        own = jnp.broadcast_to(own, (rows, rows))
        before = jnp.broadcast_to(before, (rows, rows))
        key_doc = jnp.where(lower(rows), own, before)
        bias_ref[...] = jnp.where(key_doc == own.T, 0.0, NEG)

    @pl.when(step < steps)
    def _():
        tri = lower(HALF)
        for head in range(q_ref.shape[1] // HD):
            cols = pl.ds(head * HD, HD)
            for qb in range(2):
                qs = pl.ds(qb * HALF, HALF)
                ks = pl.ds((1 - qb) * HALF, HALF)
                q = q_ref[qs, cols]
                diagonal = jnp.where(tri, nt(q, k_ref[qs, cols]), nt(q, kp_ref[qs, cols]))
                if qb == 0:
                    scores = jnp.concatenate([diagonal, nt(q, kp_ref[ks, cols])], 1)
                else:
                    scores = jnp.concatenate([nt(q, k_ref[ks, cols]), diagonal], 1)
                scores = scores * scaling + bias_ref[qs, :]
                row_max = jnp.max(scores, axis=1, keepdims=True)
                exponent = jnp.exp(scores - row_max)
                row_sum = jnp.sum(exponent, axis=1, keepdims=True)
                prob = exponent * (1.0 / row_sum)
                w_ref[head, qs, :] = prob.astype(jnp.bfloat16)
                mine = prob[:, qb * HALF : (qb + 1) * HALF]
                rest = prob[:, (1 - qb) * HALF : (2 - qb) * HALF].astype(jnp.bfloat16)
                mine_own = jnp.where(tri, mine, 0.0).astype(jnp.bfloat16)
                mine_before = jnp.where(tri, 0.0, mine).astype(jnp.bfloat16)
                att = nn(mine_own, v_ref[qs, cols]) + nn(mine_before, vp_ref[qs, cols])
                att = att + nn(rest, (vp_ref if qb == 0 else v_ref)[ks, cols])
                att_ref[qs, cols] = att.astype(jnp.bfloat16)

    for j in range(steps):

        @pl.when(step == j)
        def _():
            all_ref[j] = att_ref[...]

    @pl.when(step >= steps)
    def _():
        wide = PAIR * HD
        out = nn(all_ref[0], far_ref[:wide, :])
        for j in range(1, steps):
            out += nn(all_ref[j], far_ref[j * wide : (j + 1) * wide, :])
        out = out.astype(jnp.bfloat16)
        far0_ref[...] = out[:HALF]
        far1_ref[...] = out[HALF:]


def cost(flops, moved, transcendentals=0):
    return pl.CostEstimate(flops=int(flops * COST), bytes_accessed=int(moved * COST), transcendentals=int(transcendentals * COST))


ANY = pl.BlockSpec(memory_space=pl.ANY)


def corner(x):
    block = (1,) * (x.ndim - 2) + (16, HD)
    return pl.BlockSpec(block, lambda *_: (0,) * x.ndim)


def call(kernel, index, grid, blocked, after, out_specs, out_shape, moved, flops, name, scratch=(), aliases=None):
    count = len(blocked)
    waits = len(after)
    outs = len(out_shape)

    def run(index_ref, *refs):
        kernel(index_ref, *refs[:count], *refs[count + waits : count + waits + outs], *refs[count + waits + outs + 1 :])
        refs[count + waits + outs][0, 0] = jnp.float32(0.0)

    result = pl.pallas_call(
        run,
        grid_spec=pltpu.PrefetchScalarGridSpec(
            num_scalar_prefetch=1,
            grid=grid,
            in_specs=[spec for _, spec in blocked] + [corner(x) for x in after],
            out_specs=list(out_specs) + [pl.BlockSpec((1, 1), lambda *_: (0, 0), memory_space=pltpu.SMEM)],
            scratch_shapes=list(scratch),
        ),
        out_shape=list(out_shape) + [jax.ShapeDtypeStruct((1, 1), jnp.float32)],
        input_output_aliases=aliases or {},
        compiler_params=params(),
        cost_estimate=cost(flops, moved),
        name=name,
    )(index, *[x for x, _ in blocked], *after)
    return result[:-1], result[-1].reshape(())


def tie(index, after):
    _, zero = call(lambda index_ref: None, index, (1,), [], after, [], [], 8192, 0, "tie")
    return zero


def forward(index, doc, q, k, v, kp, vp, weight):
    rows, feature = q.shape
    pairs = feature // HD // PAIR
    block = 512
    width = weight.shape[1] // 4
    blocks = width // block
    head = pl.BlockSpec((rows, PAIR * HD), lambda n, *_: (0, jnp.minimum(n, pairs - 1)))
    late = lambda n: jnp.maximum(n - pairs, 0)
    far = pl.BlockSpec((HALF, block), lambda n, *_: (0, late(n)))
    out = jax.ShapeDtypeStruct((HALF, width), jnp.bfloat16)
    return call(
        functools.partial(forward_kernel, pairs), index, (pairs + blocks,),
        [(doc, pl.BlockSpec(doc.shape, lambda n, *_: (0, 0)))] + [(x, head) for x in (q, k, v, kp, vp)]
        + [(weight, pl.BlockSpec((feature, block), lambda n, idx: (0, idx[0] * blocks + late(n))))], [],
        [head, pl.BlockSpec((PAIR, rows, rows), lambda n, *_: (jnp.minimum(n, pairs - 1), 0, 0)), far, far],
        [jax.ShapeDtypeStruct((rows, feature), jnp.bfloat16), jax.ShapeDtypeStruct((PAIR * pairs, rows, rows), jnp.bfloat16), out, out],
        2**23, 12 * 2 * 2**23 * PAIR * pairs, "attend",
        scratch=[pltpu.VMEM((rows, rows), jnp.float32), pltpu.VMEM((pairs, rows, PAIR * HD), jnp.bfloat16)],
    )


def project(weight, index, groups, total, after):
    rows = sum(piece[0].shape[0] for piece in groups[0])
    depth = groups[0][0][0].shape[1]
    out_rows = weight.shape[0]
    block = 256
    shape = [[(len(piece), piece[0].shape[0]) for piece in g] for g in groups]
    has_total = total is not None

    def kernel(index_ref, *refs):
        refs = list(refs)
        w = [refs.pop(0)[...] for _ in groups]
        out_ref = refs[-1]
        start = 0
        base = refs[-2] if has_total else None
        sums = {}
        for j, pieces in enumerate(shape):
            start = 0
            for many, height in pieces:
                x = refs.pop(0)[...]
                for _ in range(many - 1):
                    x = x + refs.pop(0)[...]
                term = nt(x, w[j])
                key = (start, height)
                at = pl.ds(start, height)
                if j == 0:
                    out_ref[at, :] = term + base[at, :] if has_total else term
                else:
                    out_ref[at, :] += term
                start += height

    blocked = [(weight, pl.BlockSpec((block, depth), lambda n, idx, j=j: (n, idx[j]))) for j in range(len(groups))]
    for g in groups:
        for piece in g:
            for x in piece:
                blocked.append((x, pl.BlockSpec(x.shape, lambda n, idx: (0, 0))))
    if has_total:
        blocked.append((total, pl.BlockSpec((rows, block), lambda n, idx: (0, n))))
    return call(
        kernel, index, (out_rows // block,), blocked, after,
        [pl.BlockSpec((rows, block), lambda n, idx: (0, n))],
        [jax.ShapeDtypeStruct((rows, out_rows), jnp.float32)],
        2 * out_rows * depth * len(groups), 2 * rows * depth * out_rows * len(groups), "project",
    )


def parts(weight, index, attended, count, after, stream=None):
    rows, depth = attended.shape
    width = weight.shape[1] // 4
    block = 512
    steps = width // block

    def kernel(index_ref, x_ref, *refs):
        base = count + (stream is not None)
        for j in range(count):
            out = nn(x_ref[...], refs[j][...])
            if stream is not None and j == count - 1:
                out = refs[count][...].astype(jnp.float32) - out
            out = out.astype(jnp.bfloat16)
            refs[base + 2 * j][...] = out[:HALF]
            refs[base + 2 * j + 1][...] = out[HALF:]

    blocked = [(attended, pl.BlockSpec((rows, depth), lambda n, idx: (0, 0)))]
    for j in range(count):
        blocked.append((weight, pl.BlockSpec((depth, block), lambda n, idx, j=j: (0, idx[j] * steps + n))))
    if stream is not None:
        blocked.append((stream, pl.BlockSpec((rows, block), lambda n, idx: (0, n))))
    return call(
        kernel, index, (steps,), blocked, after,
        [pl.BlockSpec((HALF, block), lambda n, idx: (0, n))] * (2 * count),
        [jax.ShapeDtypeStruct((HALF, width), jnp.bfloat16)] * (2 * count),
        count * 2 * depth * width, 2 * rows * depth * width * count, "parts",
    )


def place(index, whole, rows, piece, start, after):
    height, width = piece.shape
    blocked = [(piece, pl.BlockSpec((height, width), lambda n, idx: (0, 0)))]
    aliases = None
    if whole is not None:
        blocked.append((whole, ANY))
        aliases = {2: 0}

    def kernel(index_ref, x_ref, *refs):
        refs[-1][...] = x_ref[...]

    (out,), zero = call(
        kernel, index, (1,), blocked, after,
        [pl.BlockSpec((height, width), lambda n, idx: (start // height, 0))],
        [jax.ShapeDtypeStruct((rows, width), piece.dtype)],
        4 * height * width, 0, "place", aliases=aliases,
    )
    return out, zero


def settle(index, which, grads, k, v, back, after):
    height, width = k.shape
    wide = 512

    def kernel(index_ref, k_ref, v_ref, back_ref, *refs):
        gk_ref, gv_ref = refs[-2:]
        gk_ref[...] = (k_ref[...].astype(jnp.float32) + back_ref[0].astype(jnp.float32)).astype(jnp.bfloat16)
        gv_ref[...] = (v_ref[...].astype(jnp.float32) + back_ref[1].astype(jnp.float32)).astype(jnp.bfloat16)

    flat = pl.BlockSpec((height, wide), lambda n, idx: (0, n))
    out_spec = pl.BlockSpec((height, wide), lambda n, idx: (which, n))
    out = jax.ShapeDtypeStruct((2 * height, width), jnp.bfloat16)
    return call(
        kernel, index, (width // wide,),
        [(k, flat), (v, flat), (back, pl.BlockSpec((2, height, wide), lambda n, idx: (0, 0, n)))] + [(x, ANY) for x in grads],
        after, [out_spec, out_spec], [out, out],
        16 * height * width, 0, "settle", aliases={4: 0, 5: 1} if grads else None,
    )


def gate(index, x, after):
    (out,), _ = call(
        lambda *refs: None, index, (1,), [(x, ANY)], after, [ANY], [jax.ShapeDtypeStruct(x.shape, x.dtype)], 8192, 0, "gate", aliases={1: 0}
    )
    return out


def total_of(*terms):
    result = terms[0].astype(jnp.float32)
    for x in terms[1:]:
        result = result + x.astype(jnp.float32)
    return result


def backward(qb, weight, index, total, outer, middle, probs, attended, q, k, v, kp, vp, carried, after, steps, earlier=()):
    rows, feature = q.shape
    heads = feature // HD
    depth = outer.shape[1]
    wide = PAIR * HD
    scaling = HD ** (-0.5)
    bf = jnp.bfloat16
    first = steps[0]
    kept = list(earlier) if earlier else list(carried[:1])
    skip = len(after) + len(kept)

    def kernel(index_ref, w_ref, total_ref, outer_ref, middle_ref, p_ref, att_ref, q_ref, k_ref, v_ref, kp_ref, vp_ref, *refs):
        refs = refs[skip:]
        carry = refs[:4] if qb else ()
        dq_ref, send_ref, k0_ref, v0_ref, k1_ref, v1_ref, x_ref = refs[len(carry) :]

        @pl.when((pl.program_id(0) == 0) & (index_ref[1] == 1))
        def _():
            x_ref[...] = outer_ref[...]

        @pl.when((pl.program_id(0) == 0) & (index_ref[1] == 0))
        def _():
            x_ref[...] = middle_ref[...]

        qs = pl.ds(qb * HALF, HALF)
        ks = pl.ds((1 - qb) * HALF, HALF)
        tri = lower(HALF)
        d_out_pair = (total_ref[...] + nt(x_ref[...], w_ref[...])).astype(bf)
        for head in range(PAIR):
            cols = pl.ds(head * HD, HD)
            d_out = d_out_pair[:, head * HD : (head + 1) * HD]
            row_delta = jnp.sum(
                d_out.astype(jnp.float32) * att_ref[:, cols].astype(jnp.float32), axis=1, keepdims=True
            )
            qh = q_ref[:, cols]
            k_rest_ref, v_rest_ref = (k_ref, v_ref) if qb else (kp_ref, vp_ref)
            k_rest, v_rest = k_rest_ref[ks, cols], v_rest_ref[ks, cols]
            own, prev = (qs, pl.ds(0, HALF)) if qb else (pl.ds(0, HALF), qs)
            p_diag = p_ref[head, :, qb * HALF : (qb + 1) * HALF].astype(jnp.float32)
            p_rest = p_ref[head, :, (1 - qb) * HALF : (2 - qb) * HALF]
            dp_diag = jnp.where(tri, nt(d_out, v_ref[own, cols]), nt(d_out, vp_ref[prev, cols]))
            dp_rest = nt(d_out, v_rest)
            ds_diag = p_diag * (dp_diag - row_delta)
            ds_rest = (p_rest.astype(jnp.float32) * (dp_rest - row_delta)).astype(bf)
            ds_own = jnp.where(tri, ds_diag, 0.0).astype(bf)
            ds_before = jnp.where(tri, 0.0, ds_diag).astype(bf)
            p_own = jnp.where(tri, p_diag, 0.0).astype(bf)
            p_before = jnp.where(tri, 0.0, p_diag).astype(bf)
            dq = nn(ds_own, k_ref[own, cols]) + nn(ds_before, kp_ref[prev, cols]) + nn(ds_rest, k_rest)
            dq_ref[:, cols] = (dq * scaling).astype(bf)
            dk_own, dv_own = tn(ds_own, qh) * scaling, tn(p_own, d_out)
            dk_before, dv_before = tn(ds_before, qh) * scaling, tn(p_before, d_out)
            dk_rest, dv_rest = tn(ds_rest, qh) * scaling, tn(p_rest, d_out)
            if qb == 0:
                send_ref[0, :, cols] = dk_before.astype(bf)
                send_ref[1, :, cols] = dv_before.astype(bf)
                k0_ref[:, cols], v0_ref[:, cols] = dk_own.astype(bf), dv_own.astype(bf)
                k1_ref[:, cols], v1_ref[:, cols] = dk_rest.astype(bf), dv_rest.astype(bf)
            else:
                k0i, v0i, kri, vri = carry
                send_ref[0, :, cols] = (dk_before + kri[:, cols].astype(jnp.float32)).astype(bf)
                send_ref[1, :, cols] = (dv_before + vri[:, cols].astype(jnp.float32)).astype(bf)
                k0_ref[:, cols] = (dk_rest + k0i[:, cols].astype(jnp.float32)).astype(bf)
                v0_ref[:, cols] = (dv_rest + v0i[:, cols].astype(jnp.float32)).astype(bf)
                k1_ref[:, cols], v1_ref[:, cols] = dk_own.astype(bf), dv_own.astype(bf)

    whole = pl.BlockSpec((rows, wide), lambda h, *_: (0, first + h))
    half = pl.BlockSpec((HALF, wide), lambda h, *_: (0, first + h))
    mine = pl.BlockSpec((HALF, wide), lambda h, *_: (qb, first + h))
    blocked = [
        (weight, pl.BlockSpec((wide, depth), lambda h, idx: (first + h, idx[0]))),
        (total, mine),
        (outer, pl.BlockSpec((HALF, depth), lambda h, *_: (0, 0))),
        (middle, pl.BlockSpec((HALF, depth), lambda h, *_: (qb, 0))),
        (probs, pl.BlockSpec((PAIR, HALF, rows), lambda h, *_: (first + h, qb, 0))),
        (attended, mine),
        (q, mine),
        (k, whole if qb else mine),
        (v, whole if qb else mine),
        (kp, mine if qb else whole),
        (vp, mine if qb else whole),
    ]
    aliases = {1 + len(blocked) + i: i for i in range(len(kept))}
    pair = pl.BlockSpec((2, HALF, wide), lambda h, *_: (0, 0, first + h))
    blocked += [(x, ANY) for x in kept] + [(x, corner(x)) for x in after] + [(x, half) for x in carried[1:]]
    half_out = jax.ShapeDtypeStruct((HALF, feature), bf)
    whole_out = jax.ShapeDtypeStruct((rows, feature), bf)
    return call(
        kernel, index, (steps[1] - first,), blocked, [],
        [mine, pair] + [half] * 4,
        [whole_out, jax.ShapeDtypeStruct((2, HALF, feature), bf)] + [half_out] * 4,
        16 * 2**20, 2 * HALF * depth * feature * 3, "backward", aliases=aliases,
        scratch=[pltpu.VMEM((HALF, depth), bf)],
    )


def from_behind(block, axis, distance):
    devices = range(lax.axis_size(axis))
    route = [(i - distance, i) for i in devices if i - distance in devices]
    return lax.ppermute(block, axis, route)


def shifted(block, axis, distance):
    count = lax.axis_size(axis)
    return lax.ppermute(block, axis, [((i - distance) % count, i) for i in range(count)])


def hop(block, pairs, name):
    with jax.named_scope(name):
        return lax.ppermute(block, "tp", pairs)


def body(queries, keys, values, stream, grad_stream, out_proj, doc_ids):
    q, k, v, weight = queries[0], keys[0], values[0], out_proj[0]
    grad = grad_stream[0]
    rows, feature = q.shape
    chunks = rows // HALF
    me = lax.axis_index("tp").astype(jnp.int32)
    ctx = lax.axis_index("ctx").astype(jnp.int32)
    near, across, far = me ^ 1, me ^ 2, 3 - me
    one = lambda x: x.reshape(1)

    idx = one(me)
    end = (me == 0) | (me == 3)
    bf = jnp.bfloat16
    half = lambda x, c: x[c * HALF : (c + 1) * HALF]
    both = range(chunks)

    kp = from_behind(k, "ctx", 1)
    vp = from_behind(v, "ctx", 1)
    o1 = hop(grad, OUTER, "outer1")
    m1 = hop(grad, MIDDLE, "middle1")
    grad_next = shifted(grad, "pipe", -1)
    (attended, probs, *pa), zero = forward(jnp.stack([far, ctx]), doc_ids, q, k, v, kp, vp, weight)
    o1 = gate(idx, o1, [attended])
    m2 = hop(o1, MIDDLE, "middle2")
    to_x2 = []
    for c in both:
        to_x2.append(total_of(jnp.where(end, pa[c], half(m1, c)), zero).astype(bf))
        zero = tie(idx, [to_x2[c]])
    x2 = [hop(x, OUTER, f"outer2{'ab'[c]}") for c, x in enumerate(to_x2)]
    (pb0, pb1, pc0, pc1, pd0, pd1), _ = parts(weight, jnp.stack([across, near, me]), attended, 3, to_x2, stream[0])
    pb, pc, pd = (pb0, pb1), (pc0, pc1), (pd0, pd1)
    (total,), zero = project(weight, jnp.stack([me, near]), [[(grad,)], [(o1,)]], None, [pb0])
    n3, x3 = [], []
    for c in both:
        to_n3 = total_of(pb[c], x2[c], zero).astype(bf)
        to_x3 = total_of(jnp.where(end, pb[c], half(m2, c)), zero).astype(bf)
        n3.append(hop(to_n3, MIDDLE, f"middle3{'ab'[c]}"))
        x3.append(hop(to_x3, OUTER, f"outer3{'ab'[c]}"))
        if c == 0:
            zero = tie(idx, [to_n3, to_x3])
    (total,), zero = project(
        weight, one(across), [[(jnp.where(end, x2[c], half(m2, c)),) for c in both]], total, [to_n3, to_x3]
    )
    next_grad, zero = place(idx, None, 2 * HALF, grad_next, 0, [total])
    far_and_end = jnp.stack([far, end.astype(jnp.int32)])
    hops = {}

    def launch(p, zero):
        at, height = PIECES[p]
        c = at // HALF
        piece = slice(at - c * HALF, at - c * HALF + height)
        to_f4 = total_of(pc[c][piece], n3[c][piece], zero).astype(bf)
        to_n4 = total_of(pa[c][piece], x3[c][piece], zero).astype(bf)
        hops[p] = (hop(to_f4, OUTER, f"outer4{'abcd'[p]}"), hop(to_n4, MIDDLE, f"middle4{'abcd'[p]}"))
        return [to_f4, to_n4]

    arrived, done = [], []

    def finish(p, zero):
        at, height = PIECES[p]
        c = at // HALF
        own = pd[c][at - c * HALF : at - c * HALF + height]
        rebuilt = (own.astype(jnp.float32) - total_of(*hops[p], zero)).astype(bf)
        arrived.append(shifted(rebuilt, "pipe", -1))
        done.append(rebuilt)
        return tie(idx, [rebuilt])

    pairs = feature // HD // PAIR
    run = lambda c, *rest: backward(c, weight, far_and_end, total, x3[c], m1, probs, attended, q, k, v, kp, vp, *rest)
    sends = launch(0, zero)
    (dq, send0, k0, v0, k1, v1), zero = run(0, (), sends, (0, pairs))
    back0 = from_behind(send0, "ctx", -1)
    zero = tie(idx, [n3[1], x3[1], dq])
    sends = launch(1, zero)
    (dq, send1, k0, v0, k1, v1), zero = run(1, (dq, k0, v0, k1, v1), sends, (0, pairs))
    zero = finish(0, zero)
    grads, zero = settle(idx, 0, [], k0, v0, back0, [done[0]])
    zero = tie(idx, launch(2, zero))
    zero = finish(1, zero)
    back1 = from_behind(gate(idx, send1, [done[1]]), "ctx", -1)
    finish(2, zero)
    stream_next, zero = place(idx, None, 2 * HALF, arrived[0], 0, [done[2]])
    (grad_keys, grad_values), _ = settle(idx, 1, grads, k1, v1, back1, [stream_next])
    after = [grad_keys]
    for (at, height), piece in list(zip(PIECES, arrived))[1:]:
        stream_next, _ = place(idx, stream_next, 2 * HALF, piece, at, after)
        after = []
    return tuple(x[None] for x in (dq, grad_keys, grad_values, stream_next, next_grad))


def solution(mesh):
    cut = P("pipe", "ctx", "tp")
    in_specs = (cut, cut, cut, cut, cut, P("pipe", "tp", None), P("pipe", None))
    out_specs = (cut, cut, cut, cut, cut)
    return jax.shard_map(body, mesh=mesh, in_specs=in_specs, out_specs=out_specs, check_vma=False)
```
